32 devices in a mesh: groups: 2 (over y), section: 8 (over z, x), shard: 2 (over core).
Axes of the slice: x: 2, y: 2, z: 4, core: 2. Of those that a mesh axis runs over, the one named last changes fastest.
Arguments:
- sent_acts: bfloat16 [4096, 3072], P(('groups', 'section', 'shard')), parts along dimension 0, may hold values from -6 to 6
- sent_grads: bfloat16 [4096, 3072], P(('groups', 'section', 'shard')), parts along dimension 0, may hold values from -6 to 6
- stashed: bfloat16 [4096, 3072], P(('groups', 'section', 'shard')), parts along dimension 0, may hold values from -6 to 6
- w_qkv: bfloat16 [8, 3072, 192], P('section', 'shard'), may hold values from -0.109375 to 0.109375
- w_proj: bfloat16 [8, 64, 3072], P('section', None, 'shard'), may hold values from -0.75 to 0.75
- neighbour: int32 [32], P(('groups', 'section', 'shard')), parts along dimension 0, may hold values from 0 to 1
Outputs:
- next_acts: bfloat16 [4096, 3072], P(('groups', 'section', 'shard')), parts along dimension 0
- next_grads: bfloat16 [4096, 3072], P(('groups', 'section', 'shard')), parts along dimension 0
- grad_qkv: bfloat16 [16, 3072, 192], P(('groups', 'section'), 'shard'), parts along dimension 0
- grad_proj: bfloat16 [16, 64, 3072], P(('groups', 'section'), None, 'shard'), parts along dimension 0
The draws below stay inside these ranges and needn't reach their ends.
There are 2 independent parts, one for each index of `groups`. The reference program is written for one: setup_inputs(seed, part) draws one part's arguments, and reference() takes and returns one part's arrays. A program takes and returns all parts, laid end to end along the dimension named above; an argument that names none is the same for every part. Nothing has to cross between parts.
Inputs may be any that keep to these rules, and one draw needn't show every extreme that they name: `neighbour`: a block number within the same section's 2 blocks.
All inputs are finite; a program needn't handle non-finite values.
Results may differ from the reference program's by a relative error of at most 0.0099.
Values may be sent and summed in bfloat16 or wider, within the bound.
No kernel may reach another device: no remote copies, remote signals or barrier semaphores. Data moves between devices by JAX's collectives and lax.ppermute only.
A program may use at most 64 MiB of HBM per device.

```python
import jax
import jax.numpy as jnp
from jax import lax

D = 3072
HS = 64
BLK = 128
PAIRB = 2
ROWS = 2048
N_SECTION = 8


def touch_ends(drawn, rng, least, largest):
    longest = drawn.shape.index(max(drawn.shape))
    spots = []
    for shift in (0, 1):
        where = [jax.random.randint(jax.random.fold_in(rng, axis), (), 0, length) for axis, length in enumerate(drawn.shape)]
        where[longest] = (where[longest] + shift) % drawn.shape[longest]
        spots.append(tuple(where))
    return drawn.at[spots[0]].set(least).at[spots[1]].set(largest)


def steps_of(key, dims, shards, smallest, largest):
    factor_of, own = 1.0, jax.random.fold_in(key, 6)
    for dim, blocks in shards:
        steps = jnp.exp(jax.random.uniform(jax.random.fold_in(own, dim), (blocks,), jnp.float32, smallest / len(shards), largest / len(shards)))
        factor_of = factor_of * jnp.repeat(steps, dims[dim] // blocks).reshape([-1 if axis == dim else 1 for axis in range(len(dims))])
    return factor_of


def noise(rng, dims, scale, limit, split=(), held_as=jnp.bfloat16):
    factor_of = steps_of(rng, dims, split, -0.22, 0.18) if split else 1.0
    values = jax.random.normal(rng, dims, jnp.float32) * scale * factor_of
    return jnp.minimum(jnp.maximum(values, -limit), limit).astype(held_as)


def setup_inputs(seed: int = 0, part: int = 0) -> dict:
    arg_keys = jax.random.split(jax.random.key(seed), 7)
    part_keys = jax.random.split(jax.random.fold_in(arg_keys[6], part), 7)
    sent_acts = noise(part_keys[0], (ROWS, D), 1.0, 6.0, ((0, 16),))
    sent_grads = noise(part_keys[1], (ROWS, D), 1.0, 6.0, ((0, 16),))
    stashed = noise(part_keys[2], (ROWS, D), 1.0, 6.0, ((0, 16),))
    w_qkv = noise(arg_keys[3], (N_SECTION, D, 3 * HS), D ** -0.5, 0.109375, ((0, 8), (1, 2)))
    w_proj = noise(arg_keys[4], (N_SECTION, HS, D), HS ** -0.5, 0.75, ((0, 8), (2, 2)))
    neighbour = touch_ends(jax.random.randint(part_keys[5], (N_SECTION * PAIRB,), 0, PAIRB), jax.random.fold_in(part_keys[5], 1), 0, PAIRB - 1).astype(jnp.int32)
    return {"sent_acts": sent_acts, "sent_grads": sent_grads, "stashed": stashed, "w_qkv": w_qkv, "w_proj": w_proj, "neighbour": neighbour}


EPSILON = 1e-05

def normalize(token_rows):
    widened = token_rows.astype(jnp.float32)
    inverse_rms = lax.rsqrt(lax.optimization_barrier(jnp.mean(widened * widened, axis=-1, keepdims=True)) + EPSILON)
    return (widened, inverse_rms, (widened * inverse_rms).astype(jnp.bfloat16))

def batch_stacked(pattern, first_op, second_op):
    first_op, second_op = lax.optimization_barrier((first_op, second_op))
    return jnp.einsum(pattern, first_op.astype(jnp.float32), second_op.astype(jnp.float32))

def collect(onehot, parts):
    return jnp.einsum('bp,bkh->pkh', onehot, parts, precision=lax.Precision.HIGHEST)

def attend(query_rows, key_blocks, value_blocks, own_index, near_index):
    softmax_scale = HS ** (-0.5)
    local_key_rows = key_blocks[own_index]
    neighbour_key_rows = key_blocks[near_index]
    local_value_rows = value_blocks[own_index]
    neighbour_value_rows = value_blocks[near_index]
    tiled_copies = (near_index == own_index)[:, None, None]
    local_exponent = jnp.exp(batch_stacked('ljn,len->lje', query_rows, local_key_rows) * softmax_scale)
    neighbour_exponent = jnp.where(tiled_copies, 0.0, jnp.exp(batch_stacked('ljn,len->lje', query_rows, neighbour_key_rows) * softmax_scale))
    denominator = lax.optimization_barrier(jnp.sum(local_exponent, axis=-1, keepdims=True)) + lax.optimization_barrier(jnp.sum(neighbour_exponent, axis=-1, keepdims=True))
    soft_own = local_exponent / denominator
    soft_near = neighbour_exponent / denominator
    local_low_precision = soft_own.astype(jnp.bfloat16)
    neighbour_low_precision = soft_near.astype(jnp.bfloat16)
    attention_output = batch_stacked('lwy,lyo->lwo', local_low_precision, local_value_rows) + batch_stacked('lwy,lyo->lwo', neighbour_low_precision, neighbour_value_rows)
    return (attention_output.astype(jnp.bfloat16), (soft_own, soft_near, local_low_precision, neighbour_low_precision))

def attend_back(attention_output_gradient, query_rows, key_blocks, value_blocks, own_index, near_index, soft_parts):
    soft_own, soft_near, local_low_precision, neighbour_low_precision = soft_parts
    softmax_scale = HS ** (-0.5)
    local_key_rows = key_blocks[own_index]
    neighbour_key_rows = key_blocks[near_index]
    local_value_rows = value_blocks[own_index]
    neighbour_value_rows = value_blocks[near_index]
    local_softmax_gradient = batch_stacked('ljn,len->lje', attention_output_gradient, local_value_rows)
    neighbour_softmax_gradient = batch_stacked('ljn,len->lje', attention_output_gradient, neighbour_value_rows)
    shared = lax.optimization_barrier(jnp.sum(soft_own * local_softmax_gradient, axis=-1, keepdims=True)) + lax.optimization_barrier(jnp.sum(soft_near * neighbour_softmax_gradient, axis=-1, keepdims=True))
    local_score_gradient = (soft_own * (local_softmax_gradient - shared) * softmax_scale).astype(jnp.bfloat16)
    neighbour_score_gradient = (soft_near * (neighbour_softmax_gradient - shared) * softmax_scale).astype(jnp.bfloat16)
    query_gradient = batch_stacked('lwy,lyo->lwo', local_score_gradient, local_key_rows) + batch_stacked('lwy,lyo->lwo', neighbour_score_gradient, neighbour_key_rows)
    local_key_gradient = batch_stacked('mde,mdu->meu', local_score_gradient, query_rows)
    neighbour_key_gradient = batch_stacked('mde,mdu->meu', neighbour_score_gradient, query_rows)
    local_value_gradient = batch_stacked('mde,mdu->meu', local_low_precision, attention_output_gradient)
    neighbour_value_gradient = batch_stacked('mde,mdu->meu', neighbour_low_precision, attention_output_gradient)
    labels = jnp.arange(key_blocks.shape[0], dtype=jnp.int32)
    onehot_own = (own_index[:, None] == labels[None, :]).astype(jnp.float32)
    onehot_near = (near_index[:, None] == labels[None, :]).astype(jnp.float32)
    dkeys = collect(onehot_own, local_key_gradient) + collect(onehot_near, neighbour_key_gradient)
    dvalues = collect(onehot_own, local_value_gradient) + collect(onehot_near, neighbour_value_gradient)
    return (query_gradient, dkeys, dvalues)

def prepare(token_rows, section_qkv, near_index):
    widened, inverse_rms, normed = normalize(token_rows)
    projected = jnp.dot(normed, section_qkv, preferred_element_type=jnp.float32).astype(jnp.bfloat16)
    block_count = token_rows.shape[0] // BLK
    query_rows = projected[:, :HS].reshape(block_count, BLK, HS)
    key_blocks = projected[:, HS:2 * HS].reshape(block_count, BLK, HS)
    value_blocks = projected[:, 2 * HS:].reshape(block_count, BLK, HS)
    own_index = jnp.arange(block_count, dtype=jnp.int32)
    attention_output, soft_parts = attend(query_rows, key_blocks, value_blocks, own_index, near_index)
    attention_output = attention_output.reshape(token_rows.shape[0], HS)
    return (widened, inverse_rms, normed, query_rows, key_blocks, value_blocks, own_index, attention_output, soft_parts)

def backward_section(prepared, incoming, section_qkv, section_proj, near_index):
    widened, inverse_rms, normed, query_rows, key_blocks, value_blocks, own_index, attention_output, soft_parts = prepared
    total_rows = widened.shape[0]
    attention_output_gradient = jnp.dot(incoming, section_proj.T, preferred_element_type=jnp.float32).astype(jnp.bfloat16)
    query_gradient, dkeys, dvalues = attend_back(attention_output_gradient.reshape(-1, BLK, HS), query_rows, key_blocks, value_blocks, own_index, near_index, soft_parts)
    dprojected = jnp.concatenate([query_gradient.reshape(total_rows, HS), dkeys.reshape(total_rows, HS), dvalues.reshape(total_rows, HS)], axis=1).astype(jnp.bfloat16)
    grad_weights = jnp.dot(normed.T, dprojected, preferred_element_type=jnp.float32).astype(jnp.bfloat16)
    grad_output = jnp.dot(attention_output.T, incoming, preferred_element_type=jnp.float32).astype(jnp.bfloat16)
    dnormed = jnp.dot(dprojected, section_qkv.T, preferred_element_type=jnp.float32)
    mean_term = lax.optimization_barrier(jnp.mean(dnormed * widened, axis=-1, keepdims=True))
    dwidened = inverse_rms * dnormed - widened * inverse_rms ** 3 * mean_term
    grad_input = (incoming.astype(jnp.float32) + dwidened).astype(jnp.bfloat16)
    return (grad_input, grad_weights, grad_output)

def reference(sent_acts, sent_grads, stashed, w_qkv, w_proj, neighbour):
    pair_rows = sent_acts.shape[0] // N_SECTION
    features = sent_acts.shape[1]
    received = jnp.roll(sent_acts.reshape(N_SECTION, pair_rows, features), 1, axis=0)
    incoming = jnp.roll(sent_grads.reshape(N_SECTION, pair_rows, features), -1, axis=0)
    section_stash = stashed.reshape(N_SECTION, pair_rows, features)
    near_all = neighbour.reshape(N_SECTION, -1)

    def section_step(pieces):
        forward_rows, stash_rows, grad_rows, section_qkv, section_proj, near_index = pieces
        ahead = prepare(forward_rows, section_qkv, near_index)
        output = (ahead[0] + jnp.dot(ahead[7], section_proj, preferred_element_type=jnp.float32)).astype(jnp.bfloat16)
        behind = prepare(stash_rows, section_qkv, near_index)
        grad_input, grad_weights, grad_output = backward_section(behind, grad_rows, section_qkv, section_proj, near_index)
        return (output, grad_input, grad_weights, grad_output)
    next_acts, next_grads, grad_qkv, grad_proj = lax.map(section_step, (received, section_stash, incoming, w_qkv, w_proj, near_all))
    return (next_acts.reshape(-1, features), next_grads.reshape(-1, features), grad_qkv, grad_proj)
```

```python
import functools

import jax
import jax.numpy as jnp
from jax import lax
from jax.experimental import pallas as pl
from jax.experimental.pallas import tpu as pltpu
from jax.sharding import PartitionSpec as P

HS = 64
BLK = 128
EPSILON = 1e-05
SCALE = HS**-0.5
VMEM_LIMIT = 16 * 1024 * 1024
COST = pl.CostEstimate(flops=1024, bytes_accessed=4 * 1024 * 1024, transcendentals=0)


def passed_on(value, near):
    count = lax.axis_size("section")
    steps = (1, -1) if near else (-1, 1)
    pairs = [(source, (source + steps[source % 2]) % count) for source in range(count)]
    return lax.ppermute(value, "section", pairs)


def swapped(value):
    count = lax.axis_size("shard")
    return lax.ppermute(value, "shard", [(core, (core + 1) % count) for core in range(count)])


def dot_nn(first_op, second_op):
    return jnp.dot(first_op, second_op, preferred_element_type=jnp.float32)


def dot_nt(first_op, second_op):
    return lax.dot_general(
        first_op, second_op, (((1,), (1,)), ((), ())), preferred_element_type=jnp.float32
    )


def dot_tn(first_op, second_op):
    return lax.dot_general(
        first_op, second_op, (((0,), (0,)), ((), ())), preferred_element_type=jnp.float32
    )


def halves(core_ref, half):
    core = core_ref[0]
    return (
        pl.ds(pl.multiple_of(core * half, half), half),
        pl.ds(pl.multiple_of((1 - core) * half, half), half),
    )


def in_vmem(values):
    return [pltpu.with_memory_space_constraint(value, pltpu.VMEM) for value in values]


def in_hbm(values):
    return [pltpu.with_memory_space_constraint(value, pltpu.HBM) for value in values]


def pick_kernel(parity_ref, even_rows_ref, odd_rows_ref, *refs):
    *outs, sems = refs
    pieces = sems.shape[0]
    each = pieces // len(outs)
    step = outs[0].shape[0] // each

    def copy_from(source_ref):
        copies = []
        for piece in range(pieces):
            copies.append(
                pltpu.make_async_copy(
                    source_ref.at[pl.ds(piece * step, step)],
                    outs[piece // each].at[pl.ds(piece % each * step, step)],
                    sems.at[piece],
                )
            )
            copies[-1].start()
        for copy in copies:
            copy.wait()

    @pl.when(parity_ref[0] == 0)
    def _():
        copy_from(even_rows_ref)

    @pl.when(parity_ref[0] == 1)
    def _():
        copy_from(odd_rows_ref)


def picked(parity, even_rows, odd_rows, count):
    rows, features = even_rows.shape
    pieces = 4
    return pl.pallas_call(
        pick_kernel,
        out_shape=[pltpu.VMEM((rows // count, features), even_rows.dtype)] * count,
        in_specs=[pl.BlockSpec(memory_space=pltpu.SMEM)]
        + [pl.BlockSpec(memory_space=pl.ANY)] * 2,
        out_specs=[pl.BlockSpec(memory_space=pltpu.VMEM)] * count,
        scratch_shapes=[pltpu.SemaphoreType.DMA((pieces,))],
        compiler_params=pltpu.CompilerParams(vmem_limit_bytes=VMEM_LIMIT),
        cost_estimate=COST,
        name="pick",
    )(parity, *in_hbm((even_rows, odd_rows)))


def by_rows(refs):
    first, pairs = 0, []
    for ref in refs:
        pairs.append((pl.ds(first, ref.shape[0]), ref))
        first += ref.shape[0]
    return pairs


def stash_kernel(
    core_ref,
    own_ref,
    other_ref,
    qkv_mine_ref,
    qkv_other_ref,
    proj_mine_ref,
    projected_ref,
    normed_ref,
    wide_ref,
    inverse_ref,
    kept_own_ref,
    kept_qkv_ref,
    kept_proj_ref,
):
    kept_own_ref[...] = own_ref[...]
    kept_qkv_ref[...] = qkv_mine_ref[...]
    kept_proj_ref[...] = proj_mine_ref[...]
    half = qkv_mine_ref.shape[1]
    mine, others = halves(core_ref, half)
    for index, (rows, rows_ref) in enumerate(by_rows((own_ref, other_ref))):
        widened = rows_ref[...].astype(jnp.float32)
        inverse = lax.rsqrt(jnp.mean(widened * widened, axis=-1, keepdims=True) + EPSILON)
        normed_mine = (rows_ref[:, mine].astype(jnp.float32) * inverse).astype(jnp.bfloat16)
        normed_others = (rows_ref[:, others].astype(jnp.float32) * inverse).astype(jnp.bfloat16)
        normed_ref[rows, :] = normed_mine
        projected = dot_nt(normed_mine, qkv_mine_ref[...]) + dot_nt(
            normed_others, qkv_other_ref[...]
        )
        projected_ref[rows, :] = projected.astype(jnp.bfloat16)
        if index == 0:
            wide_ref[...] = projected
            inverse_ref[...] = inverse


def attend_kernel(
    core_ref, near_ref, near_other_ref, projected_ref, soft_ref, attended_ref, reads_ref
):
    core = core_ref[0]
    reads_ref[...] = jnp.full(reads_ref.shape, (near_ref[0] != core).astype(jnp.float32))
    keys = projected_ref[:, HS : 2 * HS]
    values = projected_ref[:, 2 * HS :]
    for index, reads_both in enumerate((near_ref[0] != core, near_other_ref[0] != 1 - core)):
        rows = pl.ds(index * BLK, BLK)
        scores = dot_nt(projected_ref[rows, :HS], keys) * SCALE
        column = lax.broadcasted_iota(jnp.int32, scores.shape, 1)
        own_block = (column >= index * BLK) & (column < (index + 1) * BLK)
        exponent = jnp.where(own_block | reads_both, jnp.exp(scores), 0.0)
        soft = exponent / jnp.sum(exponent, axis=-1, keepdims=True)
        soft_ref[rows, :] = soft
        attended_ref[rows, :] = dot_nn(soft.astype(jnp.bfloat16), values).astype(jnp.bfloat16)


def arrive_kernel(backward, count, core_ref, parity_ref, *refs):
    arrived, refs = refs[:count], refs[count:]
    qkv_mine_ref, qkv_other_ref, proj_mine_ref, proj_other_ref, *refs = refs
    local_ref, shared_ref, *half_refs = refs
    half = qkv_mine_ref.shape[1]
    mine, others = halves(core_ref, half)

    @pl.when(parity_ref[0] == backward)
    def _():
        for rows, rows_ref in by_rows(arrived):
            grad_attended = (
                dot_nt(rows_ref[:, mine], proj_mine_ref[...])
                + dot_nt(rows_ref[:, others], proj_other_ref[...])
            ).astype(jnp.bfloat16)
            local_ref[rows, :] = grad_attended
            shared_ref[rows, :HS] = grad_attended
            shared_ref[rows, HS:] = grad_attended
        for rows_ref, half_ref in zip(arrived, half_refs):
            half_ref[...] = rows_ref[:, others]

    @pl.when(parity_ref[0] != backward)
    def _():
        for half_ref in half_refs:
            half_ref[...] = jnp.zeros_like(half_ref)
        for rows, rows_ref in by_rows(arrived):
            widened = rows_ref[...].astype(jnp.float32)
            inverse = lax.rsqrt(jnp.mean(widened * widened, axis=-1, keepdims=True) + EPSILON)
            projected = (
                inverse
                * (
                    dot_nt(rows_ref[:, mine], qkv_mine_ref[...])
                    + dot_nt(rows_ref[:, others], qkv_other_ref[...])
                )
            ).astype(jnp.bfloat16)
            local_ref[rows, :] = projected[:, :HS]
            shared_ref[rows, :] = projected[:, HS:]


def own_kernel(backward, count, core_ref, parity_ref, *refs):
    arrived, refs = refs[:count], refs[count:]
    local_ref, shared_ref, projected_ref, soft_ref, attended_ref, *refs = refs
    pairs_ref, queries_ref, proj_ref = refs
    mine, _ = halves(core_ref, proj_ref.shape[1])

    @pl.when(parity_ref[0] == backward)
    def _():
        dqueries, dkeys, dvalues = back_through(
            local_ref[...], soft_ref[:BLK], projected_ref[:BLK, :HS], projected_ref
        )
        queries_ref[...] = dqueries
        pairs_ref[:, :HS] = dkeys
        pairs_ref[:, HS:] = dvalues
        proj_ref[...] = sum(
            dot_tn(attended_ref[rows, :], rows_ref[:, mine]) for rows, rows_ref in by_rows(arrived)
        )

    @pl.when(parity_ref[0] != backward)
    def _():
        pairs_ref[:BLK] = jnp.exp(dot_nt(local_ref[...], shared_ref[:, :HS]) * SCALE)


def back_through(grad_attended, soft, queries, projected_ref):
    slope = dot_nt(grad_attended, projected_ref[:, 2 * HS :])
    shared = jnp.sum(soft * slope, axis=-1, keepdims=True)
    dscore = (soft * (slope - shared) * SCALE).astype(jnp.bfloat16)
    return (
        dot_nn(dscore, projected_ref[:, HS : 2 * HS]),
        dot_tn(dscore, queries),
        dot_tn(soft.astype(jnp.bfloat16), grad_attended),
    )


def finish_kernel(backward, count, aliased, core_ref, parity_ref, *refs):
    arrived, others, refs = refs[:count], refs[count : 2 * count], refs[2 * count :]
    reads_ref, *refs = refs
    ins, outs, scratch = refs[:17], refs[17 + aliased : 21 + aliased], refs[21 + aliased :]

    @pl.when(parity_ref[0] == backward)
    def _():
        finish_backward(arrived, others, core_ref, *ins, *outs[1:], *scratch)

    @pl.when(parity_ref[0] != backward)
    def _():
        finish_forward(arrived, core_ref, reads_ref, *ins[:6], outs[0], scratch[0], scratch[3])


def finish_forward(
    arrived,
    core_ref,
    reads_ref,
    pairs_ref,
    shared_other_ref,
    local_ref,
    shared_ref,
    proj_mine_ref,
    proj_other_ref,
    next_acts_ref,
    rows_ref,
    sems,
):
    half = proj_mine_ref.shape[1]
    mine, others = halves(core_ref, half)
    own = pairs_ref[:BLK]
    near = jnp.exp(dot_nt(local_ref[...], shared_other_ref[:, :HS]) * SCALE)
    near = jnp.where(reads_ref[:1] > 0.0, near, 0.0)
    denominator = jnp.sum(own, axis=-1, keepdims=True) + jnp.sum(near, axis=-1, keepdims=True)
    attended = (
        dot_nn((own / denominator).astype(jnp.bfloat16), shared_ref[:, HS:])
        + dot_nn((near / denominator).astype(jnp.bfloat16), shared_other_ref[:, HS:])
    ).astype(jnp.bfloat16)
    copies = []
    for index, (columns, proj_ref) in enumerate(((mine, proj_mine_ref), (others, proj_other_ref))):
        added = dot_nn(attended, proj_ref[...])
        for rows, piece_ref in by_rows(arrived):
            part = added[rows.start : rows.start + rows.size]
            rows_ref[rows, columns] = (
                piece_ref[:, columns].astype(jnp.float32) + part
            ).astype(jnp.bfloat16)
        copies.append(
            pltpu.make_async_copy(
                rows_ref.at[:, columns], next_acts_ref.at[:, columns], sems.at[index]
            )
        )
        copies[-1].start()
    for copy in copies:
        copy.wait()


def finish_backward(
    arrived,
    arrived_other,
    core_ref,
    pairs_ref,
    shared_other_ref,
    local_ref,
    shared_ref,
    proj_mine_ref,
    proj_other_ref,
    dqueries_ref,
    part_proj_ref,
    qkv_mine_ref,
    qkv_other_ref,
    stashed_ref,
    projected_ref,
    soft_ref,
    attended_ref,
    normed_ref,
    wide_ref,
    inverse_ref,
    next_grads_ref,
    grad_qkv_ref,
    grad_proj_ref,
    rows_ref,
    qkv_ref,
    proj_ref,
    sems,
):
    half = qkv_mine_ref.shape[1]
    features = 2 * half
    mine, others = halves(core_ref, half)
    dqueries, dkeys, dvalues = back_through(
        shared_other_ref[:, :HS], soft_ref[BLK:], projected_ref[BLK:, :HS], projected_ref
    )
    dprojected = jnp.concatenate(
        [
            jnp.concatenate([dqueries_ref[...], dqueries], axis=0),
            dkeys + pairs_ref[:, :HS],
            dvalues + pairs_ref[:, HS:],
        ],
        axis=1,
    ).astype(jnp.bfloat16)
    own = dprojected[:BLK]
    mean_term = (
        jnp.sum(own.astype(jnp.float32) * wide_ref[...], axis=-1, keepdims=True) / features
    )
    inverse = inverse_ref[...]
    pull = inverse * inverse * mean_term
    copies = []
    for index, (columns, qkv_part_ref) in enumerate(
        ((mine, qkv_mine_ref), (others, qkv_other_ref))
    ):
        added = inverse * dot_nn(own, qkv_part_ref[...]) - pull * stashed_ref[:, columns].astype(
            jnp.float32
        )
        for rows, piece_ref in by_rows(arrived):
            part = added[rows.start : rows.start + rows.size]
            rows_ref[rows, columns] = (
                piece_ref[:, columns].astype(jnp.float32) + part
            ).astype(jnp.bfloat16)
        copies.append(
            pltpu.make_async_copy(
                rows_ref.at[:, columns], next_grads_ref.at[:, columns], sems.at[index]
            )
        )
        copies[-1].start()
    qkv_ref[...] = dot_tn(dprojected, normed_ref[...]).astype(jnp.bfloat16)
    copies.append(pltpu.make_async_copy(qkv_ref, grad_qkv_ref, sems.at[2]))
    copies[-1].start()
    proj_ref[...] = (
        part_proj_ref[...]
        + sum(
            dot_tn(attended_ref[pl.ds(BLK + rows.start, rows.size), :], piece_ref[...])
            for rows, piece_ref in by_rows(arrived_other)
        )
    ).astype(jnp.bfloat16)
    copies.append(pltpu.make_async_copy(proj_ref, grad_proj_ref, sems.at[3]))
    copies[-1].start()
    for copy in copies:
        copy.wait()


def on_device(kernel, scalars, values, outputs, name):
    return pl.pallas_call(
        kernel,
        out_shape=[pltpu.VMEM(shape, dtype) for shape, dtype in outputs],
        in_specs=[pl.BlockSpec(memory_space=pltpu.SMEM)] * len(scalars)
        + [pl.BlockSpec(memory_space=pltpu.VMEM)] * len(values),
        out_specs=[pl.BlockSpec(memory_space=pltpu.VMEM)] * len(outputs),
        compiler_params=pltpu.CompilerParams(vmem_limit_bytes=VMEM_LIMIT),
        cost_estimate=COST,
        name=name,
    )(*scalars, *in_vmem(values))


def per_device(sent_acts, sent_grads, stashed, w_qkv, w_proj, neighbour):
    bf16, f32 = jnp.bfloat16, jnp.float32
    rows, features = stashed.shape
    half = features // 2
    core = lax.axis_index("shard").astype(jnp.int32).reshape(1)
    parity = (lax.axis_index("section").astype(jnp.int32) & 1).reshape(1)
    near_rows = picked(parity, sent_acts, sent_grads, 1)[0]
    near = [passed_on(near_rows, True)]
    far_rows = picked(parity, sent_grads, sent_acts, 2)
    far = [passed_on(piece, False) for piece in far_rows]
    stashed, qkv_mine, proj_mine, neighbour, near_rows = lax.optimization_barrier(
        (stashed, w_qkv[0].T, w_proj[0], neighbour, near_rows)
    )
    stashed_other, qkv_other = swapped(stashed), swapped(qkv_mine)
    proj_other, near_other = swapped(proj_mine), swapped(neighbour)
    near_own = swapped(near_other)
    projected, normed, wide, inverse, stashed, qkv_mine, proj_mine = on_device(
        stash_kernel,
        (core,),
        (stashed, stashed_other, qkv_mine, qkv_other, proj_mine),
        [
            ((2 * rows, 3 * HS), bf16),
            ((2 * rows, half), bf16),
            ((rows, 3 * HS), f32),
            ((rows, 1), f32),
            ((rows, features), bf16),
            ((3 * HS, half), bf16),
            ((HS, half), bf16),
        ],
        "stash",
    )
    soft, attended, reads = on_device(
        attend_kernel,
        (core, near_own, near_other),
        (projected,),
        [((2 * rows, 2 * rows), f32), ((2 * rows, HS), bf16), ((8, rows), f32)],
        "attend",
    )
    results, ready = (), soft
    for backward, arrived in ((1, far), (0, near)):
        *arrived, ready = lax.optimization_barrier((*arrived, ready))
        count = len(arrived)
        local, shared, *others = on_device(
            functools.partial(arrive_kernel, backward, count),
            (core, parity),
            (*arrived, qkv_mine, qkv_other, proj_mine, proj_other),
            [((rows, HS), bf16), ((rows, 2 * HS), bf16)] + [((rows // count, half), bf16)] * count,
            "arrive",
        )
        shared_other, *others = [swapped(value) for value in (shared, *others)]
        pairs, dqueries, part_proj = on_device(
            functools.partial(own_kernel, backward, count),
            (core, parity),
            (*arrived, local, shared, projected, soft, attended),
            [((2 * rows, 2 * HS), f32), ((rows, HS), f32), ((HS, half), f32)],
            "own",
        )
        inputs = (
            *arrived,
            *others,
            reads,
            pairs,
            shared_other,
            local,
            shared,
            proj_mine,
            proj_other,
            dqueries,
            part_proj,
            qkv_mine,
            qkv_other,
            stashed,
            projected,
            soft,
            attended,
            normed,
            wide,
            inverse,
        )
        results = pl.pallas_call(
            functools.partial(finish_kernel, backward, count, len(results)),
            out_shape=[
                jax.ShapeDtypeStruct(shape, bf16)
                for shape in ((rows, features), (rows, features), (3 * HS, half), (HS, half))
            ],
            in_specs=[pl.BlockSpec(memory_space=pltpu.SMEM)] * 2
            + [pl.BlockSpec(memory_space=pltpu.VMEM)] * len(inputs)
            + [pl.BlockSpec(memory_space=pl.ANY)] * len(results),
            out_specs=[pl.BlockSpec(memory_space=pl.ANY)] * 4,
            scratch_shapes=[
                pltpu.VMEM((rows, features), bf16),
                pltpu.VMEM((3 * HS, half), bf16),
                pltpu.VMEM((HS, half), bf16),
                pltpu.SemaphoreType.DMA((4,)),
            ],
            input_output_aliases={
                2 + len(inputs) + index: index for index in range(len(results))
            },
            compiler_params=pltpu.CompilerParams(vmem_limit_bytes=VMEM_LIMIT),
            cost_estimate=COST,
            name="finish",
        )(core, parity, *in_vmem(inputs), *results)
        ready = results[0]
    next_acts, next_grads, grad_qkv, grad_proj = results
    return (next_acts, next_grads, grad_qkv.T[None], grad_proj[None])


def solution(mesh):
    return jax.shard_map(
        per_device,
        mesh=mesh,
        in_specs=(
            P(("groups", "section", "shard"), None),
            P(("groups", "section", "shard"), None),
            P(("groups", "section", "shard"), None),
            P("section", "shard", None),
            P("section", None, "shard"),
            P(("groups", "section", "shard")),
        ),
        out_specs=(
            P(("groups", "section", "shard"), None),
            P(("groups", "section", "shard"), None),
            P(("groups", "section"), "shard", None),
            P(("groups", "section"), None, "shard"),
        ),
        check_vma=False,
    )
```

```python
import collections
import functools

import jax
import jax.numpy as jnp
from jax import lax
from jax.experimental import pallas as pl
from jax.experimental.pallas import tpu as pltpu
from jax.sharding import PartitionSpec as P

Block = collections.namedtuple(
    "Block", ["row", "size", "owned", "first", "width", "array", "at"]
)

HS = 64
BLK = 128
EPSILON = 1e-05
SCALE = HS**-0.5
VMEM_LIMIT = 16 * 1024 * 1024
LAST = 512
COST = pl.CostEstimate(flops=1024, bytes_accessed=4 * 1024 * 1024, transcendentals=0)


def passed_on(value, near):
    count = lax.axis_size("section")
    steps = (1, -1) if near else (-1, 1)
    pairs = [(source, (source + steps[source % 2]) % count) for source in range(count)]
    return lax.ppermute(value, "section", pairs)


def swapped(value):
    count = lax.axis_size("shard")
    return lax.ppermute(value, "shard", [(core, (core + 1) % count) for core in range(count)])


def dot_nn(first_op, second_op):
    return jnp.dot(first_op, second_op, preferred_element_type=jnp.float32)


def dot_nt(first_op, second_op):
    return lax.dot_general(
        first_op, second_op, (((1,), (1,)), ((), ())), preferred_element_type=jnp.float32
    )


def dot_tn(first_op, second_op):
    return lax.dot_general(
        first_op, second_op, (((0,), (0,)), ((), ())), preferred_element_type=jnp.float32
    )


def columns_of(core, block, half):
    owner = core if block.owned else 1 - core
    return pl.ds(pl.multiple_of(owner * half + block.first, 128), block.width)


def rows_of(block):
    return pl.ds(block.row, block.size)


def part_of(block, refs):
    return refs[block.array][:, block.at : block.at + block.width]


def weights_of(block, mine_ref, other_ref):
    return (mine_ref if block.owned else other_ref)[:, block.first : block.first + block.width]


def in_vmem(values):
    return [pltpu.with_memory_space_constraint(value, pltpu.VMEM) for value in values]


def in_hbm(values):
    return [pltpu.with_memory_space_constraint(value, pltpu.HBM) for value in values]


def pick_kernel(blocks, core_ref, parity_ref, even_rows_ref, odd_rows_ref, *refs):
    *outs, sems = refs
    half = even_rows_ref.shape[1] // 2

    def copy_from(source_ref):
        copies = []
        for index, block in enumerate(blocks):
            copies.append(
                pltpu.make_async_copy(
                    source_ref.at[rows_of(block), columns_of(core_ref[0], block, half)],
                    outs[block.array].at[:, block.at : block.at + block.width],
                    sems.at[index],
                )
            )
            copies[-1].start()
        for copy in copies:
            copy.wait()

    @pl.when(parity_ref[0] == 0)
    def _():
        copy_from(even_rows_ref)

    @pl.when(parity_ref[0] == 1)
    def _():
        copy_from(odd_rows_ref)


def picked(blocks, scalars, even_rows, odd_rows):
    shapes = {}
    for block in blocks:
        rows, columns = shapes.get(block.array, (0, 0))
        shapes[block.array] = (max(rows, block.size), max(columns, block.at + block.width))
    return pl.pallas_call(
        functools.partial(pick_kernel, blocks),
        out_shape=[pltpu.VMEM(shapes[array], even_rows.dtype) for array in sorted(shapes)],
        in_specs=[pl.BlockSpec(memory_space=pltpu.SMEM)] * 2
        + [pl.BlockSpec(memory_space=pl.ANY)] * 2,
        out_specs=[pl.BlockSpec(memory_space=pltpu.VMEM)] * len(shapes),
        scratch_shapes=[pltpu.SemaphoreType.DMA((len(blocks),))],
        compiler_params=pltpu.CompilerParams(vmem_limit_bytes=VMEM_LIMIT),
        cost_estimate=COST,
        name="pick",
    )(*scalars, *in_hbm((even_rows, odd_rows)))


def stash_kernel(
    core_ref,
    own_ref,
    other_ref,
    qkv_mine_ref,
    qkv_other_ref,
    proj_mine_ref,
    projected_ref,
    normed_ref,
    wide_ref,
    inverse_ref,
    kept_own_ref,
    kept_qkv_ref,
    kept_proj_ref,
):
    kept_own_ref[...] = own_ref[...]
    kept_qkv_ref[...] = qkv_mine_ref[...]
    kept_proj_ref[...] = proj_mine_ref[...]
    half = qkv_mine_ref.shape[1]
    mine, others = (
        pl.ds(pl.multiple_of(owner * half, half), half) for owner in (core_ref[0], 1 - core_ref[0])
    )
    for index, rows_ref in enumerate((own_ref, other_ref)):
        rows = pl.ds(index * BLK, BLK)
        widened = rows_ref[...].astype(jnp.float32)
        inverse = lax.rsqrt(jnp.mean(widened * widened, axis=-1, keepdims=True) + EPSILON)
        normed_mine = (rows_ref[:, mine].astype(jnp.float32) * inverse).astype(jnp.bfloat16)
        normed_others = (rows_ref[:, others].astype(jnp.float32) * inverse).astype(jnp.bfloat16)
        normed_ref[rows, :] = normed_mine
        projected = dot_nt(normed_mine, qkv_mine_ref[...]) + dot_nt(
            normed_others, qkv_other_ref[...]
        )
        projected_ref[rows, :] = projected.astype(jnp.bfloat16)
        if index == 0:
            wide_ref[...] = projected
            inverse_ref[...] = inverse


def attend_kernel(
    core_ref,
    near_ref,
    near_other_ref,
    projected_ref,
    soft_ref,
    attended_ref,
    reads_ref,
    turned_ref,
    values_ref,
    keys_ref,
    queries_ref,
):
    values_ref[...] = projected_ref[:, 2 * HS :]
    keys_ref[...] = jnp.zeros_like(keys_ref)
    keys_ref[:, :HS] = projected_ref[:, HS : 2 * HS]
    queries_ref[...] = jnp.zeros_like(queries_ref)
    queries_ref[:, HS : 2 * HS] = projected_ref[:, :HS]
    core = core_ref[0]
    reads_ref[...] = jnp.full(reads_ref.shape, (near_ref[0] != core).astype(jnp.float32))
    keys = projected_ref[:, HS : 2 * HS]
    values = projected_ref[:, 2 * HS :]
    for index, reads_both in enumerate((near_ref[0] != core, near_other_ref[0] != 1 - core)):
        rows = pl.ds(index * BLK, BLK)
        scores = dot_nt(projected_ref[rows, :HS], keys) * SCALE
        column = lax.broadcasted_iota(jnp.int32, scores.shape, 1)
        own_block = (column >= index * BLK) & (column < (index + 1) * BLK)
        exponent = jnp.where(own_block | reads_both, jnp.exp(scores), 0.0)
        soft = exponent / jnp.sum(exponent, axis=-1, keepdims=True)
        soft_ref[rows, :] = soft
        turned_ref[:, rows] = soft.T.astype(jnp.bfloat16)
        attended_ref[rows, :] = dot_nn(soft.astype(jnp.bfloat16), values).astype(jnp.bfloat16)


def arrive_kernel(backward, blocks, count, begun, ended, parity_ref, *refs):
    arrived, refs = refs[:count], refs[count:]
    qkv_mine_ref, qkv_other_ref, proj_mine_ref, proj_other_ref, attended_ref, *refs = refs
    if begun:
        sums_in_ref, squares_in_ref, *refs = refs
    first_ref, second_ref, *part_refs = refs
    row_groups = sorted({(block.row, block.size) for block in blocks})
    foreign = [block for block in blocks if not block.owned]

    def summed(term, begun_ref, width):
        sums = {}
        for block in blocks:
            part = term(block)
            sums[block.row] = sums[block.row] + part if block.row in sums else part
        for row, size in row_groups:
            if begun:
                sums[row] += begun_ref[row : row + size, :width]
        return [(pl.ds(row, size), sums[row]) for row, size in row_groups]

    @pl.when(parity_ref[0] == backward)
    def _():
        if part_refs:
            part = sum(
                dot_tn(attended_ref[rows_of(block), :], part_of(block, arrived))
                for block in foreign
            ).astype(jnp.bfloat16)
            width = part_refs[0].shape[1]
            for index, part_ref in enumerate(part_refs):
                part_ref[...] = part[:, index * width : (index + 1) * width]

        def term(block):
            return dot_nt(part_of(block, arrived), weights_of(block, proj_mine_ref, proj_other_ref))

        for rows, sums in summed(term, sums_in_ref if begun else None, HS):
            if not ended:
                first_ref[rows, :HS] = sums
                continue
            grad_attended = sums.astype(jnp.bfloat16)
            first_ref[rows, :] = grad_attended
            second_ref[rows, :HS] = grad_attended
            second_ref[rows, HS:] = grad_attended

    @pl.when(parity_ref[0] != backward)
    def _():
        for part_ref in part_refs:
            part_ref[...] = jnp.zeros_like(part_ref)

        def term(block):
            return dot_nt(part_of(block, arrived), weights_of(block, qkv_mine_ref, qkv_other_ref))

        def square(block):
            widened = part_of(block, arrived).astype(jnp.float32)
            return jnp.sum(widened * widened, axis=-1, keepdims=True)

        features = 2 * qkv_mine_ref.shape[1]
        squares = summed(square, squares_in_ref if begun else None, 1)
        for (rows, sums), (_, square_sums) in zip(
            summed(term, sums_in_ref if begun else None, 3 * HS), squares
        ):
            if not ended:
                first_ref[rows, :] = sums
                second_ref[rows, :] = square_sums
                continue
            inverse = lax.rsqrt(square_sums / features + EPSILON)
            projected = (inverse * sums).astype(jnp.bfloat16)
            first_ref[rows, :] = projected[:, :HS]
            second_ref[rows, :] = projected[:, HS:]


def own_kernel(backward, blocks, count, parity_ref, *refs):
    arrived, refs = refs[:count], refs[count:]
    local_ref, shared_ref, attended_ref, *refs = refs
    padded_refs, (part_ref, proj_ref) = refs[:5], refs[5:]

    @pl.when(parity_ref[0] == backward)
    def _():
        both, alone = back_through(0, local_ref[...], *padded_refs)
        part_ref[:BLK] = both[:BLK] + alone
        part_ref[BLK:] = both[BLK:]
        sums = {}
        for block in blocks:
            if block.owned:
                term = dot_tn(attended_ref[rows_of(block), :], part_of(block, arrived))
                key = (block.first, block.width)
                sums[key] = sums[key] + term if key in sums else term
        for (first, width), total in sums.items():
            proj_ref[:, first : first + width] = total

    @pl.when(parity_ref[0] != backward)
    def _():
        part_ref[:BLK, :BLK] = jnp.exp(dot_nt(local_ref[...], shared_ref[:, :HS]) * SCALE)


def back_through(index, grad_attended, soft_ref, turned_ref, values_ref, keys_ref, queries_ref):
    first = index * BLK
    soft = soft_ref[first : first + BLK]
    slope = dot_nt(grad_attended, values_ref[...])
    shared = jnp.sum(soft * slope, axis=-1, keepdims=True)
    dscore = (soft * (slope - shared) * SCALE).astype(jnp.bfloat16)
    padded = jnp.concatenate(
        [jnp.zeros((BLK, 2 * HS), jnp.bfloat16), grad_attended], axis=1
    )
    both = dot_tn(dscore, queries_ref[first : first + BLK]) + dot_nn(
        turned_ref[:, first : first + BLK], padded
    )
    return both, dot_nn(dscore, keys_ref[...])


def finish_kernel(backward, blocks, count, others, aliased, core_ref, parity_ref, *refs):
    arrived, refs = refs[:count], refs[count:]
    arrived_other, refs = refs[:others], refs[others:]
    reads_ref, *refs = refs
    ins, outs, scratch = refs[:19], refs[19 + aliased : 23 + aliased], refs[23 + aliased :]
    arrived = (blocks, arrived)

    @pl.when(parity_ref[0] == backward)
    def _():
        finish_backward(arrived, arrived_other, core_ref, *ins, *outs[1:], *scratch)

    @pl.when(parity_ref[0] != backward)
    def _():
        finish_forward(arrived, core_ref, reads_ref, *ins[:6], outs[0], scratch[0], scratch[3])


def add_rows(arrived, owned, core, half, rows_ref, added_of):
    blocks, refs = arrived
    for block in blocks:
        if block.owned == owned:
            columns = columns_of(core, block, half)
            rows_ref[rows_of(block), columns] = (
                part_of(block, refs).astype(jnp.float32) + added_of(block, columns)
            ).astype(jnp.bfloat16)


def half_copy(core, owned, half, rows_ref, target_ref, sem):
    owner = core if owned else 1 - core
    columns = pl.ds(pl.multiple_of(owner * half, half), half)
    return pltpu.make_async_copy(rows_ref.at[:, columns], target_ref.at[:, columns], sem)


def finish_forward(
    arrived,
    core_ref,
    reads_ref,
    part_ref,
    shared_other_ref,
    local_ref,
    shared_ref,
    proj_mine_ref,
    proj_other_ref,
    next_acts_ref,
    rows_ref,
    sems,
):
    half = proj_mine_ref.shape[1]
    core = core_ref[0]
    own = part_ref[:BLK, :BLK]
    near = jnp.exp(dot_nt(local_ref[...], shared_other_ref[:, :HS]) * SCALE)
    near = jnp.where(reads_ref[:1] > 0.0, near, 0.0)
    denominator = jnp.sum(own, axis=-1, keepdims=True) + jnp.sum(near, axis=-1, keepdims=True)
    attended = (
        dot_nn((own / denominator).astype(jnp.bfloat16), shared_ref[:, HS:])
        + dot_nn((near / denominator).astype(jnp.bfloat16), shared_other_ref[:, HS:])
    ).astype(jnp.bfloat16)

    def added_of(block, columns):
        return dot_nn(
            attended[block.row : block.row + block.size],
            weights_of(block, proj_mine_ref, proj_other_ref),
        )

    copies = []
    for index, owned in enumerate((False, True)):
        add_rows(arrived, owned, core, half, rows_ref, added_of)
        copies.append(half_copy(core, owned, half, rows_ref, next_acts_ref, sems.at[index]))
        copies[-1].start()
    for copy in copies:
        copy.wait()


def finish_backward(
    arrived,
    arrived_other,
    core_ref,
    part_ref,
    shared_other_ref,
    local_ref,
    shared_ref,
    proj_mine_ref,
    proj_other_ref,
    part_proj_ref,
    qkv_mine_ref,
    qkv_other_ref,
    stashed_ref,
    attended_ref,
    normed_ref,
    wide_ref,
    inverse_ref,
    soft_ref,
    turned_ref,
    values_ref,
    keys_ref,
    queries_ref,
    next_grads_ref,
    grad_qkv_ref,
    grad_proj_ref,
    rows_ref,
    qkv_ref,
    proj_ref,
    sems,
):
    half = qkv_mine_ref.shape[1]
    core = core_ref[0]
    both, alone = back_through(
        1, shared_other_ref[:, :HS], soft_ref, turned_ref, values_ref, keys_ref, queries_ref
    )
    dprojected = jnp.concatenate(
        [part_ref[:BLK] + both[:BLK], part_ref[BLK:] + both[BLK:] + alone], axis=0
    ).astype(jnp.bfloat16)
    own = dprojected[:BLK]
    mean_term = jnp.sum(own.astype(jnp.float32) * wide_ref[...], axis=-1, keepdims=True)
    mean_term = mean_term / (2 * half)
    inverse = inverse_ref[...]
    pull = inverse * inverse * mean_term

    def added_of(block, columns):
        rows = rows_of(block)
        mine = slice(block.row, block.row + block.size)
        dnormed = dot_nn(own[mine], weights_of(block, qkv_mine_ref, qkv_other_ref))
        widened = stashed_ref[rows, columns].astype(jnp.float32)
        return inverse[mine] * dnormed - pull[mine] * widened

    copies = []
    add_rows(arrived, True, core, half, rows_ref, added_of)
    copies.append(half_copy(core, True, half, rows_ref, next_grads_ref, sems.at[2]))
    copies[-1].start()
    qkv_ref[...] = dot_tn(dprojected, normed_ref[...]).astype(jnp.bfloat16)
    add_rows(arrived, False, core, half, rows_ref, added_of)
    copies.append(pltpu.make_async_copy(qkv_ref, grad_qkv_ref, sems.at[1]))
    copies[-1].start()
    copies.append(half_copy(core, False, half, rows_ref, next_grads_ref, sems.at[3]))
    copies[-1].start()
    width = half // len(arrived_other)
    for index, other_ref in enumerate(arrived_other):
        columns = slice(index * width, (index + 1) * width)
        proj_ref[:, columns] = (
            part_proj_ref[:, columns] + other_ref[...].astype(jnp.float32)
        ).astype(jnp.bfloat16)
    copies.append(pltpu.make_async_copy(proj_ref, grad_proj_ref, sems.at[0]))
    copies[-1].start()
    for copy in copies:
        copy.wait()


def on_device(kernel, scalars, values, outputs, name):
    return pl.pallas_call(
        kernel,
        out_shape=[pltpu.VMEM(shape, dtype) for shape, dtype in outputs],
        in_specs=[pl.BlockSpec(memory_space=pltpu.SMEM)] * len(scalars)
        + [pl.BlockSpec(memory_space=pltpu.VMEM)] * len(values),
        out_specs=[pl.BlockSpec(memory_space=pltpu.VMEM)] * len(outputs),
        compiler_params=pltpu.CompilerParams(vmem_limit_bytes=VMEM_LIMIT),
        cost_estimate=COST,
        name=name,
    )(*scalars, *in_vmem(values))


def per_device(sent_acts, sent_grads, stashed, w_qkv, w_proj, neighbour):
    bf16, f32 = jnp.bfloat16, jnp.float32
    rows, features = stashed.shape
    half = features // 2
    core = lax.axis_index("shard").astype(jnp.int32).reshape(1)
    parity = (lax.axis_index("section").astype(jnp.int32) & 1).reshape(1)
    rest = LAST
    near_blocks = [
        Block(0, rows, False, 0, half, 0, 0),
        Block(0, rows, True, 0, half - rest, 0, half),
        Block(0, rows, True, half - rest, rest, 1, 0),
    ]
    size = rows // 2
    far_blocks = [
        Block(piece * size, size, owned, 0, half, piece, half * owned)
        for piece in range(2)
        for owned in (False, True)
    ]
    near_pieces = picked(near_blocks, (core, parity), sent_acts, sent_grads)
    near = [passed_on(piece, True) for piece in near_pieces]
    far_pieces = picked(far_blocks, (core, parity), sent_grads, sent_acts)
    far = [passed_on(piece, False) for piece in far_pieces]
    stashed, qkv_mine, proj_mine, neighbour, _ = lax.optimization_barrier(
        (stashed, w_qkv[0].T, w_proj[0], neighbour, near_pieces[0])
    )
    stashed_other, qkv_other = swapped(stashed), swapped(qkv_mine)
    proj_other, near_other = swapped(proj_mine), swapped(neighbour)
    near_own = swapped(near_other)
    projected, normed, wide, inverse, stashed, qkv_mine, proj_mine = on_device(
        stash_kernel,
        (core,),
        (stashed, stashed_other, qkv_mine, qkv_other, proj_mine),
        [
            ((2 * rows, 3 * HS), bf16),
            ((2 * rows, half), bf16),
            ((rows, 3 * HS), f32),
            ((rows, 1), f32),
            ((rows, features), bf16),
            ((3 * HS, half), bf16),
            ((HS, half), bf16),
        ],
        "stash",
    )
    soft, attended, reads, *padded = on_device(
        attend_kernel,
        (core, near_own, near_other),
        (projected,),
        [
            ((2 * rows, 2 * rows), f32),
            ((2 * rows, HS), bf16),
            ((8, rows), f32),
            ((2 * rows, 2 * rows), bf16),
            ((2 * rows, HS), bf16),
            ((2 * rows, 3 * HS), bf16),
            ((2 * rows, 3 * HS), bf16),
        ],
        "attend",
    )
    results, ready = (), soft
    weights = (qkv_mine, qkv_other, proj_mine, proj_other, attended)
    parts = [((HS, half // 2), bf16)] * 2
    given = [((rows, HS), bf16), ((rows, 2 * HS), bf16)]
    for backward, blocks, arrived in ((1, far_blocks, far), (0, near_blocks, near)):
        count = len(arrived)
        if backward:
            *arrived, ready = lax.optimization_barrier((*arrived, ready))
            local, shared, *others = on_device(
                functools.partial(arrive_kernel, backward, blocks, count, False, True),
                (parity,),
                (*arrived, *weights),
                given + parts,
                "arrive",
            )
            others = [swapped(piece) for piece in others]
        else:
            early, last = arrived
            early, ready = lax.optimization_barrier((early, ready))
            sums, squares, *others = on_device(
                functools.partial(arrive_kernel, backward, blocks[:-1], 1, False, False),
                (parity,),
                (early, *weights),
                [((rows, 3 * HS), f32), ((rows, 1), f32)] + parts,
                "begin",
            )
            others = [swapped(piece) for piece in others]
            last_block = [blocks[-1]._replace(array=0)]
            last, sums = lax.optimization_barrier((last, sums))
            local, shared = on_device(
                functools.partial(arrive_kernel, backward, last_block, 1, True, True),
                (parity,),
                (last, *weights, sums, squares),
                given,
                "arrive",
            )
            arrived = [early, last]
        shared_other = swapped(shared)
        part, part_proj = on_device(
            functools.partial(own_kernel, backward, blocks, count),
            (parity,),
            (*arrived, local, shared, attended, soft, *padded),
            [((2 * rows, 3 * HS), f32), ((HS, half), f32)],
            "own",
        )
        inputs = (
            *arrived,
            *others,
            reads,
            part,
            shared_other,
            local,
            shared,
            proj_mine,
            proj_other,
            part_proj,
            qkv_mine,
            qkv_other,
            stashed,
            attended,
            normed,
            wide,
            inverse,
            soft,
            *padded,
        )
        results = pl.pallas_call(
            functools.partial(
                finish_kernel, backward, blocks, count, len(others), len(results)
            ),
            out_shape=[
                jax.ShapeDtypeStruct(shape, bf16)
                for shape in ((rows, features), (rows, features), (3 * HS, half), (HS, half))
            ],
            in_specs=[pl.BlockSpec(memory_space=pltpu.SMEM)] * 2
            + [pl.BlockSpec(memory_space=pltpu.VMEM)] * len(inputs)
            + [pl.BlockSpec(memory_space=pl.ANY)] * len(results),
            out_specs=[pl.BlockSpec(memory_space=pl.ANY)] * 4,
            scratch_shapes=[
                pltpu.VMEM((rows, features), bf16),
                pltpu.VMEM((3 * HS, half), bf16),
                pltpu.VMEM((HS, half), bf16),
                pltpu.SemaphoreType.DMA((4,)),
            ],
            input_output_aliases={
                2 + len(inputs) + index: index for index in range(len(results))
            },
            compiler_params=pltpu.CompilerParams(vmem_limit_bytes=VMEM_LIMIT),
            cost_estimate=COST,
            name="finish",
        )(core, parity, *in_vmem(inputs), *results)
        ready = results[0]
    next_acts, next_grads, grad_qkv, grad_proj = results
    return (next_acts, next_grads, grad_qkv.T[None], grad_proj[None])


def solution(mesh):
    return jax.shard_map(
        per_device,
        mesh=mesh,
        in_specs=(
            P(("groups", "section", "shard"), None),
            P(("groups", "section", "shard"), None),
            P(("groups", "section", "shard"), None),
            P("section", "shard", None),
            P("section", None, "shard"),
            P(("groups", "section", "shard")),
        ),
        out_specs=(
            P(("groups", "section", "shard"), None),
            P(("groups", "section", "shard"), None),
            P(("groups", "section"), "shard", None),
            P(("groups", "section"), None, "shard"),
        ),
        check_vma=False,
    )
```

```python
import collections
import functools

import jax
import jax.numpy as jnp
from jax import lax
from jax.experimental import pallas as pl
from jax.experimental.pallas import tpu as pltpu
from jax.sharding import PartitionSpec as P

Block = collections.namedtuple(
    "Block", ["row", "size", "owned", "first", "width", "array", "at"]
)

HS = 64
BLK = 128
EPSILON = 1e-05
SCALE = HS**-0.5
VMEM_LIMIT = 16 * 1024 * 1024
LAST = 256
COST = pl.CostEstimate(flops=1024, bytes_accessed=4 * 1024 * 1024, transcendentals=0)


def passed_on(value, near):
    count = lax.axis_size("section")
    steps = (1, -1) if near else (-1, 1)
    pairs = [(source, (source + steps[source % 2]) % count) for source in range(count)]
    return lax.ppermute(value, "section", pairs)


def swapped(value):
    count = lax.axis_size("shard")
    return lax.ppermute(value, "shard", [(core, (core + 1) % count) for core in range(count)])


def dot_nn(first_op, second_op):
    return jnp.dot(first_op, second_op, preferred_element_type=jnp.float32)


def dot_nt(first_op, second_op):
    return lax.dot_general(
        first_op, second_op, (((1,), (1,)), ((), ())), preferred_element_type=jnp.float32
    )


def dot_tn(first_op, second_op):
    return lax.dot_general(
        first_op, second_op, (((0,), (0,)), ((), ())), preferred_element_type=jnp.float32
    )


def columns_of(core, block, half):
    owner = core if block.owned else 1 - core
    return pl.ds(pl.multiple_of(owner * half + block.first, 128), block.width)


def rows_of(block):
    return pl.ds(block.row, block.size)


def part_of(block, refs):
    return refs[block.array][:, block.at : block.at + block.width]


def weights_of(block, mine_ref, other_ref):
    return (mine_ref if block.owned else other_ref)[:, block.first : block.first + block.width]


def in_vmem(values):
    return [pltpu.with_memory_space_constraint(value, pltpu.VMEM) for value in values]


def in_hbm(values):
    return [pltpu.with_memory_space_constraint(value, pltpu.HBM) for value in values]


def pick_kernel(blocks, core_ref, parity_ref, even_rows_ref, odd_rows_ref, *refs):
    *outs, sems = refs
    half = even_rows_ref.shape[1] // 2

    def copy_from(source_ref):
        copies = []
        for index, block in enumerate(blocks):
            copies.append(
                pltpu.make_async_copy(
                    source_ref.at[rows_of(block), columns_of(core_ref[0], block, half)],
                    outs[block.array].at[:, block.at : block.at + block.width],
                    sems.at[index],
                )
            )
            copies[-1].start()
        for copy in copies:
            copy.wait()

    @pl.when(parity_ref[0] == 0)
    def _():
        copy_from(even_rows_ref)

    @pl.when(parity_ref[0] == 1)
    def _():
        copy_from(odd_rows_ref)


def picked(blocks, scalars, even_rows, odd_rows):
    shapes = {}
    for block in blocks:
        rows, columns = shapes.get(block.array, (0, 0))
        shapes[block.array] = (max(rows, block.size), max(columns, block.at + block.width))
    return pl.pallas_call(
        functools.partial(pick_kernel, blocks),
        out_shape=[pltpu.VMEM(shapes[array], even_rows.dtype) for array in sorted(shapes)],
        in_specs=[pl.BlockSpec(memory_space=pltpu.SMEM)] * 2
        + [pl.BlockSpec(memory_space=pl.ANY)] * 2,
        out_specs=[pl.BlockSpec(memory_space=pltpu.VMEM)] * len(shapes),
        scratch_shapes=[pltpu.SemaphoreType.DMA((len(blocks),))],
        compiler_params=pltpu.CompilerParams(vmem_limit_bytes=VMEM_LIMIT),
        cost_estimate=COST,
        name="pick",
    )(*scalars, *in_hbm((even_rows, odd_rows)))


def normed_kernel(
    core_ref, rows_ref, mine_ref, others_ref, inverse_ref, kept_ref
):
    kept_ref[...] = rows_ref[...]
    half = mine_ref.shape[1]
    widened = rows_ref[...].astype(jnp.float32)
    inverse = lax.rsqrt(jnp.mean(widened * widened, axis=-1, keepdims=True) + EPSILON)
    inverse_ref[...] = inverse
    for owner, half_ref in ((core_ref[0], mine_ref), (1 - core_ref[0], others_ref)):
        columns = pl.ds(pl.multiple_of(owner * half, half), half)
        half_ref[...] = (rows_ref[:, columns].astype(jnp.float32) * inverse).astype(jnp.bfloat16)


def project_kernel(
    mine_ref,
    others_ref,
    qkv_mine_ref,
    qkv_other_ref,
    proj_mine_ref,
    projected_ref,
    wide_ref,
    kept_qkv_ref,
    kept_proj_ref,
):
    kept_qkv_ref[...] = qkv_mine_ref[...]
    kept_proj_ref[...] = proj_mine_ref[...]
    projected = dot_nt(mine_ref[...], qkv_mine_ref[...]) + dot_nt(
        others_ref[...], qkv_other_ref[...]
    )
    wide_ref[...] = projected
    projected_ref[...] = projected.astype(jnp.bfloat16)


def attend_kernel(
    core_ref,
    near_ref,
    near_other_ref,
    own_ref,
    other_ref,
    normed_own_ref,
    normed_other_ref,
    soft_ref,
    attended_ref,
    reads_ref,
    normed_ref,
    turned_ref,
    values_ref,
    keys_ref,
    queries_ref,
):
    normed_ref[:BLK] = normed_own_ref[...]
    normed_ref[BLK:] = normed_other_ref[...]
    keys_ref[...] = jnp.zeros_like(keys_ref)
    queries_ref[...] = jnp.zeros_like(queries_ref)
    for index, projected_ref in enumerate((own_ref, other_ref)):
        rows = pl.ds(index * BLK, BLK)
        keys_ref[rows, :HS] = projected_ref[:, HS : 2 * HS]
        queries_ref[rows, HS : 2 * HS] = projected_ref[:, :HS]
        values_ref[rows, :] = projected_ref[:, 2 * HS :]
    core = core_ref[0]
    reads_ref[...] = jnp.full(reads_ref.shape, (near_ref[0] != core).astype(jnp.float32))
    keys = keys_ref[:, :HS]
    for index, (projected_ref, reads_both) in enumerate(
        ((own_ref, near_ref[0] != core), (other_ref, near_other_ref[0] != 1 - core))
    ):
        rows = pl.ds(index * BLK, BLK)
        scores = dot_nt(projected_ref[:, :HS], keys) * SCALE
        column = lax.broadcasted_iota(jnp.int32, scores.shape, 1)
        own_block = (column >= index * BLK) & (column < (index + 1) * BLK)
        exponent = jnp.where(own_block | reads_both, jnp.exp(scores), 0.0)
        soft = exponent / jnp.sum(exponent, axis=-1, keepdims=True)
        soft_ref[rows, :] = soft
        turned_ref[:, rows] = soft.T.astype(jnp.bfloat16)
        attended_ref[rows, :] = dot_nn(soft.astype(jnp.bfloat16), values_ref[...]).astype(
            jnp.bfloat16
        )


def arrive_kernel(backward, blocks, count, begun, ended, parity_ref, *refs):
    arrived, refs = refs[:count], refs[count:]
    qkv_mine_ref, qkv_other_ref, proj_mine_ref, proj_other_ref, attended_ref, *refs = refs
    if begun:
        sums_in_ref, squares_in_ref, *refs = refs
    first_ref, second_ref, *part_refs = refs
    row_groups = sorted({(block.row, block.size) for block in blocks})
    foreign = [block for block in blocks if not block.owned]

    def summed(term, begun_ref, width):
        sums = {}
        for block in blocks:
            part = term(block)
            sums[block.row] = sums[block.row] + part if block.row in sums else part
        for row, size in row_groups:
            if begun:
                sums[row] += begun_ref[row : row + size, :width]
        return [(pl.ds(row, size), sums[row]) for row, size in row_groups]

    @pl.when(parity_ref[0] == backward)
    def _():
        if part_refs:
            part = sum(
                dot_tn(attended_ref[rows_of(block), :], part_of(block, arrived))
                for block in foreign
            ).astype(jnp.bfloat16)
            width = part_refs[0].shape[1]
            for index, part_ref in enumerate(part_refs):
                part_ref[...] = part[:, index * width : (index + 1) * width]

        def term(block):
            return dot_nt(part_of(block, arrived), weights_of(block, proj_mine_ref, proj_other_ref))

        for rows, sums in summed(term, sums_in_ref if begun else None, HS):
            if not ended:
                first_ref[rows, :HS] = sums
                continue
            grad_attended = sums.astype(jnp.bfloat16)
            first_ref[rows, :] = grad_attended
            second_ref[rows, :HS] = grad_attended
            second_ref[rows, HS:] = grad_attended

    @pl.when(parity_ref[0] != backward)
    def _():
        for part_ref in part_refs:
            part_ref[...] = jnp.zeros_like(part_ref)

        def term(block):
            return dot_nt(part_of(block, arrived), weights_of(block, qkv_mine_ref, qkv_other_ref))

        def square(block):
            widened = part_of(block, arrived).astype(jnp.float32)
            return jnp.sum(widened * widened, axis=-1, keepdims=True)

        features = 2 * qkv_mine_ref.shape[1]
        squares = summed(square, squares_in_ref if begun else None, 1)
        for (rows, sums), (_, square_sums) in zip(
            summed(term, sums_in_ref if begun else None, 3 * HS), squares
        ):
            if not ended:
                first_ref[rows, :] = sums
                second_ref[rows, :] = square_sums
                continue
            inverse = lax.rsqrt(square_sums / features + EPSILON)
            projected = (inverse * sums).astype(jnp.bfloat16)
            first_ref[rows, :] = projected[:, :HS]
            second_ref[rows, :] = projected[:, HS:]


def own_kernel(backward, blocks, count, parity_ref, *refs):
    arrived, refs = refs[:count], refs[count:]
    local_ref, shared_ref, attended_ref, *refs = refs
    padded_refs, (part_ref, proj_ref) = refs[:5], refs[5:]

    @pl.when(parity_ref[0] == backward)
    def _():
        both, alone = back_through(0, local_ref[...], *padded_refs)
        part_ref[:BLK] = both[:BLK] + alone
        part_ref[BLK:] = both[BLK:]
        sums = {}
        for block in blocks:
            if block.owned:
                term = dot_tn(attended_ref[rows_of(block), :], part_of(block, arrived))
                key = (block.first, block.width)
                sums[key] = sums[key] + term if key in sums else term
        for (first, width), total in sums.items():
            proj_ref[:, first : first + width] = total

    @pl.when(parity_ref[0] != backward)
    def _():
        part_ref[:BLK, :BLK] = jnp.exp(dot_nt(local_ref[...], shared_ref[:, :HS]) * SCALE)


def back_through(index, grad_attended, soft_ref, turned_ref, values_ref, keys_ref, queries_ref):
    first = index * BLK
    soft = soft_ref[first : first + BLK]
    slope = dot_nt(grad_attended, values_ref[...])
    shared = jnp.sum(soft * slope, axis=-1, keepdims=True)
    dscore = (soft * (slope - shared) * SCALE).astype(jnp.bfloat16)
    padded = jnp.concatenate(
        [jnp.zeros((BLK, 2 * HS), jnp.bfloat16), grad_attended], axis=1
    )
    both = dot_tn(dscore, queries_ref[first : first + BLK]) + dot_nn(
        turned_ref[:, first : first + BLK], padded
    )
    return both, dot_nn(dscore, keys_ref[...])


def finish_kernel(backward, blocks, count, others, aliased, core_ref, parity_ref, *refs):
    arrived, refs = refs[:count], refs[count:]
    arrived_other, refs = refs[:others], refs[others:]
    reads_ref, *refs = refs
    ins, outs, scratch = refs[:19], refs[19 + aliased : 23 + aliased], refs[23 + aliased :]
    arrived = (blocks, arrived)

    @pl.when(parity_ref[0] == backward)
    def _():
        finish_backward(arrived, arrived_other, core_ref, *ins, *outs[1:], *scratch)

    @pl.when(parity_ref[0] != backward)
    def _():
        finish_forward(arrived, core_ref, reads_ref, *ins[:6], outs[0], scratch[0], scratch[3])


def add_rows(arrived, owned, core, half, rows_ref, added_of):
    blocks, refs = arrived
    for block in blocks:
        if block.owned == owned:
            columns = columns_of(core, block, half)
            rows_ref[rows_of(block), columns] = (
                part_of(block, refs).astype(jnp.float32) + added_of(block, columns)
            ).astype(jnp.bfloat16)


def half_copy(core, owned, half, rows_ref, target_ref, sem):
    owner = core if owned else 1 - core
    columns = pl.ds(pl.multiple_of(owner * half, half), half)
    return pltpu.make_async_copy(rows_ref.at[:, columns], target_ref.at[:, columns], sem)


def finish_forward(
    arrived,
    core_ref,
    reads_ref,
    part_ref,
    shared_other_ref,
    local_ref,
    shared_ref,
    proj_mine_ref,
    proj_other_ref,
    next_acts_ref,
    rows_ref,
    sems,
):
    half = proj_mine_ref.shape[1]
    core = core_ref[0]
    own = part_ref[:BLK, :BLK]
    near = jnp.exp(dot_nt(local_ref[...], shared_other_ref[:, :HS]) * SCALE)
    near = jnp.where(reads_ref[:1] > 0.0, near, 0.0)
    denominator = jnp.sum(own, axis=-1, keepdims=True) + jnp.sum(near, axis=-1, keepdims=True)
    attended = (
        dot_nn((own / denominator).astype(jnp.bfloat16), shared_ref[:, HS:])
        + dot_nn((near / denominator).astype(jnp.bfloat16), shared_other_ref[:, HS:])
    ).astype(jnp.bfloat16)

    def added_of(block, columns):
        return dot_nn(
            attended[block.row : block.row + block.size],
            weights_of(block, proj_mine_ref, proj_other_ref),
        )

    copies = []
    for index, owned in enumerate((False, True)):
        add_rows(arrived, owned, core, half, rows_ref, added_of)
        copies.append(half_copy(core, owned, half, rows_ref, next_acts_ref, sems.at[index]))
        copies[-1].start()
    for copy in copies:
        copy.wait()


def finish_backward(
    arrived,
    arrived_other,
    core_ref,
    part_ref,
    shared_other_ref,
    local_ref,
    shared_ref,
    proj_mine_ref,
    proj_other_ref,
    part_proj_ref,
    qkv_mine_ref,
    qkv_other_ref,
    stashed_ref,
    attended_ref,
    normed_ref,
    wide_ref,
    inverse_ref,
    soft_ref,
    turned_ref,
    values_ref,
    keys_ref,
    queries_ref,
    next_grads_ref,
    grad_qkv_ref,
    grad_proj_ref,
    rows_ref,
    qkv_ref,
    proj_ref,
    sems,
):
    half = qkv_mine_ref.shape[1]
    core = core_ref[0]
    both, alone = back_through(
        1, shared_other_ref[:, :HS], soft_ref, turned_ref, values_ref, keys_ref, queries_ref
    )
    dprojected = jnp.concatenate(
        [part_ref[:BLK] + both[:BLK], part_ref[BLK:] + both[BLK:] + alone], axis=0
    ).astype(jnp.bfloat16)
    own = dprojected[:BLK]
    mean_term = jnp.sum(own.astype(jnp.float32) * wide_ref[...], axis=-1, keepdims=True)
    mean_term = mean_term / (2 * half)
    inverse = inverse_ref[...]
    pull = inverse * inverse * mean_term

    def added_of(block, columns):
        rows = rows_of(block)
        mine = slice(block.row, block.row + block.size)
        dnormed = dot_nn(own[mine], weights_of(block, qkv_mine_ref, qkv_other_ref))
        widened = stashed_ref[rows, columns].astype(jnp.float32)
        return inverse[mine] * dnormed - pull[mine] * widened

    copies = []
    add_rows(arrived, True, core, half, rows_ref, added_of)
    copies.append(half_copy(core, True, half, rows_ref, next_grads_ref, sems.at[2]))
    copies[-1].start()
    qkv_ref[...] = dot_tn(dprojected, normed_ref[...]).astype(jnp.bfloat16)
    add_rows(arrived, False, core, half, rows_ref, added_of)
    copies.append(pltpu.make_async_copy(qkv_ref, grad_qkv_ref, sems.at[1]))
    copies[-1].start()
    copies.append(half_copy(core, False, half, rows_ref, next_grads_ref, sems.at[3]))
    copies[-1].start()
    width = half // len(arrived_other)
    for index, other_ref in enumerate(arrived_other):
        columns = slice(index * width, (index + 1) * width)
        proj_ref[:, columns] = (
            part_proj_ref[:, columns] + other_ref[...].astype(jnp.float32)
        ).astype(jnp.bfloat16)
    copies.append(pltpu.make_async_copy(proj_ref, grad_proj_ref, sems.at[0]))
    copies[-1].start()
    for copy in copies:
        copy.wait()


def on_device(kernel, scalars, values, outputs, name):
    return pl.pallas_call(
        kernel,
        out_shape=[pltpu.VMEM(shape, dtype) for shape, dtype in outputs],
        in_specs=[pl.BlockSpec(memory_space=pltpu.SMEM)] * len(scalars)
        + [pl.BlockSpec(memory_space=pltpu.VMEM)] * len(values),
        out_specs=[pl.BlockSpec(memory_space=pltpu.VMEM)] * len(outputs),
        compiler_params=pltpu.CompilerParams(vmem_limit_bytes=VMEM_LIMIT),
        cost_estimate=COST,
        name=name,
    )(*scalars, *in_vmem(values))


def per_device(sent_acts, sent_grads, stashed, w_qkv, w_proj, neighbour):
    bf16, f32 = jnp.bfloat16, jnp.float32
    rows, features = stashed.shape
    half = features // 2
    core = lax.axis_index("shard").astype(jnp.int32).reshape(1)
    parity = (lax.axis_index("section").astype(jnp.int32) & 1).reshape(1)
    rest = LAST
    near_blocks = [
        Block(0, rows, False, 0, half, 0, 0),
        Block(0, rows, True, 0, half - rest, 0, half),
        Block(0, rows, True, half - rest, rest, 1, 0),
    ]
    size = rows // 2
    far_blocks = [
        Block(piece * size, size, owned, 0, half, piece, half * owned)
        for piece in range(2)
        for owned in (False, True)
    ]
    near_pieces = picked(near_blocks, (core, parity), sent_acts, sent_grads)
    near = [passed_on(piece, True) for piece in near_pieces]
    far_pieces = picked(far_blocks, (core, parity), sent_grads, sent_acts)
    far = [passed_on(piece, False) for piece in far_pieces]
    stashed, qkv_mine, proj_mine, neighbour, _ = lax.optimization_barrier(
        (stashed, w_qkv[0].T, w_proj[0], neighbour, near_pieces[0])
    )
    normed_mine, normed_others, inverse, stashed = on_device(
        normed_kernel,
        (core,),
        (stashed,),
        [
            ((rows, half), bf16),
            ((rows, half), bf16),
            ((rows, 1), f32),
            ((rows, features), bf16),
        ],
        "norm",
    )
    normed_other, qkv_other = swapped(normed_others), swapped(qkv_mine)
    proj_other, near_other = swapped(proj_mine), swapped(neighbour)
    near_own = swapped(near_other)
    projected, wide, qkv_mine, proj_mine = on_device(
        project_kernel,
        (),
        (normed_mine, normed_others, qkv_mine, qkv_other, proj_mine),
        [
            ((rows, 3 * HS), bf16),
            ((rows, 3 * HS), f32),
            ((3 * HS, half), bf16),
            ((HS, half), bf16),
        ],
        "project",
    )
    soft, attended, reads, normed, *padded = on_device(
        attend_kernel,
        (core, near_own, near_other),
        (projected, swapped(projected), normed_mine, normed_other),
        [
            ((2 * rows, 2 * rows), f32),
            ((2 * rows, HS), bf16),
            ((8, rows), f32),
            ((2 * rows, half), bf16),
            ((2 * rows, 2 * rows), bf16),
            ((2 * rows, HS), bf16),
            ((2 * rows, 3 * HS), bf16),
            ((2 * rows, 3 * HS), bf16),
        ],
        "attend",
    )
    results, ready = (), soft
    weights = (qkv_mine, qkv_other, proj_mine, proj_other, attended)
    parts = [((HS, half // 2), bf16)] * 2
    given = [((rows, HS), bf16), ((rows, 2 * HS), bf16)]
    for backward, blocks, arrived in ((1, far_blocks, far), (0, near_blocks, near)):
        count = len(arrived)
        if backward:
            *arrived, ready = lax.optimization_barrier((*arrived, ready))
            local, shared, *others = on_device(
                functools.partial(arrive_kernel, backward, blocks, count, False, True),
                (parity,),
                (*arrived, *weights),
                given + parts,
                "arrive",
            )
            others = [swapped(piece) for piece in others]
        else:
            early, last = arrived
            early, ready = lax.optimization_barrier((early, ready))
            sums, squares, *others = on_device(
                functools.partial(arrive_kernel, backward, blocks[:-1], 1, False, False),
                (parity,),
                (early, *weights),
                [((rows, 3 * HS), f32), ((rows, 1), f32)] + parts,
                "begin",
            )
            others = [swapped(piece) for piece in others]
            last_block = [blocks[-1]._replace(array=0)]
            last, sums = lax.optimization_barrier((last, sums))
            local, shared = on_device(
                functools.partial(arrive_kernel, backward, last_block, 1, True, True),
                (parity,),
                (last, *weights, sums, squares),
                given,
                "arrive",
            )
            arrived = [early, last]
        shared_other = swapped(shared)
        part, part_proj = on_device(
            functools.partial(own_kernel, backward, blocks, count),
            (parity,),
            (*arrived, local, shared, attended, soft, *padded),
            [((2 * rows, 3 * HS), f32), ((HS, half), f32)],
            "own",
        )
        inputs = (
            *arrived,
            *others,
            reads,
            part,
            shared_other,
            local,
            shared,
            proj_mine,
            proj_other,
            part_proj,
            qkv_mine,
            qkv_other,
            stashed,
            attended,
            normed,
            wide,
            inverse,
            soft,
            *padded,
        )
        results = pl.pallas_call(
            functools.partial(
                finish_kernel, backward, blocks, count, len(others), len(results)
            ),
            out_shape=[
                jax.ShapeDtypeStruct(shape, bf16)
                for shape in ((rows, features), (rows, features), (3 * HS, half), (HS, half))
            ],
            in_specs=[pl.BlockSpec(memory_space=pltpu.SMEM)] * 2
            + [pl.BlockSpec(memory_space=pltpu.VMEM)] * len(inputs)
            + [pl.BlockSpec(memory_space=pl.ANY)] * len(results),
            out_specs=[pl.BlockSpec(memory_space=pl.ANY)] * 4,
            scratch_shapes=[
                pltpu.VMEM((rows, features), bf16),
                pltpu.VMEM((3 * HS, half), bf16),
                pltpu.VMEM((HS, half), bf16),
                pltpu.SemaphoreType.DMA((4,)),
            ],
            input_output_aliases={
                2 + len(inputs) + index: index for index in range(len(results))
            },
            compiler_params=pltpu.CompilerParams(vmem_limit_bytes=VMEM_LIMIT),
            cost_estimate=COST,
            name="finish",
        )(core, parity, *in_vmem(inputs), *results)
        ready = results[0]
    next_acts, next_grads, grad_qkv, grad_proj = results
    return (next_acts, next_grads, grad_qkv.T[None], grad_proj[None])


def solution(mesh):
    return jax.shard_map(
        per_device,
        mesh=mesh,
        in_specs=(
            P(("groups", "section", "shard"), None),
            P(("groups", "section", "shard"), None),
            P(("groups", "section", "shard"), None),
            P("section", "shard", None),
            P("section", None, "shard"),
            P(("groups", "section", "shard")),
        ),
        out_specs=(
            P(("groups", "section", "shard"), None),
            P(("groups", "section", "shard"), None),
            P(("groups", "section"), "shard", None),
            P(("groups", "section"), None, "shard"),
        ),
        check_vma=False,
    )
```

```python
import collections
import functools

import jax
import jax.numpy as jnp
from jax import lax
from jax.experimental import pallas as pl
from jax.experimental.pallas import tpu as pltpu
from jax.sharding import PartitionSpec as P

Block = collections.namedtuple(
    "Block", ["row", "size", "owned", "first", "width", "array", "at"]
)

HS = 64
BLK = 128
EPSILON = 1e-05
SCALE = HS**-0.5
VMEM_LIMIT = 16 * 1024 * 1024
LAST = 256
COST = pl.CostEstimate(flops=1024, bytes_accessed=4 * 1024 * 1024, transcendentals=0)


def passed_on(value, near):
    count = lax.axis_size("section")
    steps = (1, -1) if near else (-1, 1)
    pairs = [(source, (source + steps[source % 2]) % count) for source in range(count)]
    return lax.ppermute(value, "section", pairs)


def swapped(value):
    count = lax.axis_size("shard")
    return lax.ppermute(value, "shard", [(core, (core + 1) % count) for core in range(count)])


def dot_nn(first_op, second_op):
    return jnp.dot(first_op, second_op, preferred_element_type=jnp.float32)


def dot_nt(first_op, second_op):
    return lax.dot_general(
        first_op, second_op, (((1,), (1,)), ((), ())), preferred_element_type=jnp.float32
    )


def dot_tn(first_op, second_op):
    return lax.dot_general(
        first_op, second_op, (((0,), (0,)), ((), ())), preferred_element_type=jnp.float32
    )


def columns_of(core, block, half):
    owner = core if block.owned else 1 - core
    return pl.ds(pl.multiple_of(owner * half + block.first, 128), block.width)


def rows_of(block):
    return pl.ds(block.row, block.size)


def part_of(block, refs):
    return refs[block.array][:, block.at : block.at + block.width]


def weights_of(block, mine_ref, other_ref):
    return (mine_ref if block.owned else other_ref)[:, block.first : block.first + block.width]


def in_vmem(values):
    return [pltpu.with_memory_space_constraint(value, pltpu.VMEM) for value in values]


def in_hbm(values):
    return [pltpu.with_memory_space_constraint(value, pltpu.HBM) for value in values]


def pick_kernel(blocks, core_ref, parity_ref, even_rows_ref, odd_rows_ref, *refs):
    *outs, sems = refs
    half = even_rows_ref.shape[1] // 2

    def copy_from(source_ref):
        copies = []
        for index, block in enumerate(blocks):
            copies.append(
                pltpu.make_async_copy(
                    source_ref.at[rows_of(block), columns_of(core_ref[0], block, half)],
                    outs[block.array].at[:, block.at : block.at + block.width],
                    sems.at[index],
                )
            )
            copies[-1].start()
        for copy in copies:
            copy.wait()

    @pl.when(parity_ref[0] == 0)
    def _():
        copy_from(even_rows_ref)

    @pl.when(parity_ref[0] == 1)
    def _():
        copy_from(odd_rows_ref)


def picked(blocks, scalars, even_rows, odd_rows):
    shapes = {}
    for block in blocks:
        rows, columns = shapes.get(block.array, (0, 0))
        shapes[block.array] = (max(rows, block.size), max(columns, block.at + block.width))
    return pl.pallas_call(
        functools.partial(pick_kernel, blocks),
        out_shape=[pltpu.VMEM(shapes[array], even_rows.dtype) for array in sorted(shapes)],
        in_specs=[pl.BlockSpec(memory_space=pltpu.SMEM)] * 2
        + [pl.BlockSpec(memory_space=pl.ANY)] * 2,
        out_specs=[pl.BlockSpec(memory_space=pltpu.VMEM)] * len(shapes),
        scratch_shapes=[pltpu.SemaphoreType.DMA((len(blocks),))],
        compiler_params=pltpu.CompilerParams(vmem_limit_bytes=VMEM_LIMIT),
        cost_estimate=COST,
        name="pick",
    )(*scalars, *in_hbm((even_rows, odd_rows)))


def normed_kernel(
    core_ref, rows_ref, mine_ref, others_ref, inverse_ref, kept_ref
):
    kept_ref[...] = rows_ref[...]
    half = mine_ref.shape[1]
    widened = rows_ref[...].astype(jnp.float32)
    inverse = lax.rsqrt(jnp.mean(widened * widened, axis=-1, keepdims=True) + EPSILON)
    inverse_ref[...] = inverse
    for owner, half_ref in ((core_ref[0], mine_ref), (1 - core_ref[0], others_ref)):
        columns = pl.ds(pl.multiple_of(owner * half, half), half)
        half_ref[...] = (rows_ref[:, columns].astype(jnp.float32) * inverse).astype(jnp.bfloat16)


def project_kernel(
    mine_ref,
    others_ref,
    qkv_mine_ref,
    qkv_other_ref,
    proj_mine_ref,
    projected_ref,
    wide_ref,
    kept_qkv_ref,
    kept_proj_ref,
):
    kept_qkv_ref[...] = qkv_mine_ref[...]
    kept_proj_ref[...] = proj_mine_ref[...]
    projected = dot_nt(mine_ref[...], qkv_mine_ref[...]) + dot_nt(
        others_ref[...], qkv_other_ref[...]
    )
    wide_ref[...] = projected
    projected_ref[...] = projected.astype(jnp.bfloat16)


def attend_kernel(
    core_ref,
    near_ref,
    near_other_ref,
    own_ref,
    other_ref,
    normed_own_ref,
    normed_other_ref,
    soft_ref,
    attended_ref,
    reads_ref,
    normed_ref,
    turned_ref,
    wide_ref,
    values_ref,
    keys_ref,
    queries_ref,
):
    normed_ref[:BLK] = normed_own_ref[...]
    normed_ref[BLK:] = normed_other_ref[...]
    keys_ref[...] = jnp.zeros_like(keys_ref)
    queries_ref[...] = jnp.zeros_like(queries_ref)
    for index, projected_ref in enumerate((own_ref, other_ref)):
        rows = pl.ds(index * BLK, BLK)
        keys_ref[rows, :HS] = projected_ref[:, HS : 2 * HS]
        queries_ref[rows, HS : 2 * HS] = projected_ref[:, :HS]
        values_ref[rows, :] = projected_ref[:, 2 * HS :]
    core = core_ref[0]
    reads_ref[...] = jnp.full(reads_ref.shape, (near_ref[0] != core).astype(jnp.float32))
    keys = keys_ref[:, :HS]
    for index, (projected_ref, reads_both) in enumerate(
        ((own_ref, near_ref[0] != core), (other_ref, near_other_ref[0] != 1 - core))
    ):
        rows = pl.ds(index * BLK, BLK)
        scores = dot_nt(projected_ref[:, :HS], keys) * SCALE
        column = lax.broadcasted_iota(jnp.int32, scores.shape, 1)
        own_block = (column >= index * BLK) & (column < (index + 1) * BLK)
        exponent = jnp.where(own_block | reads_both, jnp.exp(scores), 0.0)
        soft = exponent / jnp.sum(exponent, axis=-1, keepdims=True)
        soft_ref[rows, :] = soft
        turned_ref[:, rows] = soft.T.astype(jnp.bfloat16)
        rounded = soft.astype(jnp.bfloat16)
        attended = dot_nn(rounded, values_ref[...])
        attended_ref[rows, :] = attended.astype(jnp.bfloat16)
        rest = (soft - rounded.astype(jnp.float32)).astype(jnp.bfloat16)
        wide_ref[rows, :] = attended + dot_nn(rest, values_ref[...])


def arrive_kernel(backward, blocks, count, begun, ended, parity_ref, *refs):
    arrived, refs = refs[:count], refs[count:]
    qkv_mine_ref, qkv_other_ref, proj_mine_ref, proj_other_ref, attended_ref, *refs = refs
    if begun:
        sums_in_ref, squares_in_ref, *refs = refs
    first_ref, second_ref, *part_refs = refs
    row_groups = sorted({(block.row, block.size) for block in blocks})
    foreign = [block for block in blocks if not block.owned]

    def summed(term, begun_ref, width):
        sums = {}
        for block in blocks:
            part = term(block)
            sums[block.row] = sums[block.row] + part if block.row in sums else part
        for row, size in row_groups:
            if begun:
                sums[row] += begun_ref[row : row + size, :width]
        return [(pl.ds(row, size), sums[row]) for row, size in row_groups]

    @pl.when(parity_ref[0] == backward)
    def _():
        if part_refs:
            part = sum(
                dot_tn(attended_ref[rows_of(block), :], part_of(block, arrived))
                for block in foreign
            ).astype(jnp.bfloat16)
            width = part_refs[0].shape[1]
            for index, part_ref in enumerate(part_refs):
                part_ref[...] = part[:, index * width : (index + 1) * width]

        def term(block):
            return dot_nt(part_of(block, arrived), weights_of(block, proj_mine_ref, proj_other_ref))

        for rows, sums in summed(term, sums_in_ref if begun else None, HS):
            if not ended:
                first_ref[rows, :HS] = sums
                continue
            grad_attended = sums.astype(jnp.bfloat16)
            first_ref[rows, :] = grad_attended
            second_ref[rows, :HS] = grad_attended
            second_ref[rows, HS:] = grad_attended

    @pl.when(parity_ref[0] != backward)
    def _():
        for part_ref in part_refs:
            part_ref[...] = jnp.zeros_like(part_ref)

        def term(block):
            return dot_nt(part_of(block, arrived), weights_of(block, qkv_mine_ref, qkv_other_ref))

        def square(block):
            widened = part_of(block, arrived).astype(jnp.float32)
            return jnp.sum(widened * widened, axis=-1, keepdims=True)

        features = 2 * qkv_mine_ref.shape[1]
        squares = summed(square, squares_in_ref if begun else None, 1)
        for (rows, sums), (_, square_sums) in zip(
            summed(term, sums_in_ref if begun else None, 3 * HS), squares
        ):
            if not ended:
                first_ref[rows, :] = sums
                second_ref[rows, :] = square_sums
                continue
            inverse = lax.rsqrt(square_sums / features + EPSILON)
            projected = (inverse * sums).astype(jnp.bfloat16)
            first_ref[rows, :] = projected[:, :HS]
            second_ref[rows, :] = projected[:, HS:]


def own_kernel(backward, blocks, count, parity_ref, *refs):
    arrived, refs = refs[:count], refs[count:]
    local_ref, shared_ref, attended_ref, *refs = refs
    padded_refs, (part_ref, proj_ref) = refs[:6], refs[6:]

    @pl.when(parity_ref[0] == backward)
    def _():
        both, alone = back_through(0, local_ref[...], padded_refs)
        part_ref[:BLK] = both[:BLK] + alone
        part_ref[BLK:] = both[BLK:]
        sums = {}
        for block in blocks:
            if block.owned:
                term = dot_tn(attended_ref[rows_of(block), :], part_of(block, arrived))
                key = (block.first, block.width)
                sums[key] = sums[key] + term if key in sums else term
        for (first, width), total in sums.items():
            proj_ref[:, first : first + width] = total

    @pl.when(parity_ref[0] != backward)
    def _():
        part_ref[:BLK, :BLK] = jnp.exp(dot_nt(local_ref[...], shared_ref[:, :HS]) * SCALE)


def back_through(index, grad_attended, refs):
    soft_ref, turned_ref, wide_ref, values_ref, keys_ref, queries_ref = refs
    first = index * BLK
    soft = soft_ref[first : first + BLK]
    slope = dot_nt(grad_attended, values_ref[...])
    shared = jnp.sum(
        grad_attended.astype(jnp.float32) * wide_ref[first : first + BLK], axis=-1, keepdims=True
    )
    dscore = (soft * (slope - shared) * SCALE).astype(jnp.bfloat16)
    padded = jnp.concatenate([jnp.zeros((BLK, 2 * HS), jnp.bfloat16), grad_attended], axis=1)
    both = dot_tn(dscore, queries_ref[first : first + BLK]) + dot_nn(
        turned_ref[:, first : first + BLK], padded
    )
    return both, dot_nn(dscore, keys_ref[...])


def finish_kernel(backward, blocks, count, others, aliased, core_ref, parity_ref, *refs):
    arrived, refs = refs[:count], refs[count:]
    arrived_other, refs = refs[:others], refs[others:]
    reads_ref, *refs = refs
    ins, outs, scratch = refs[:20], refs[20 + aliased : 24 + aliased], refs[24 + aliased :]
    arrived = (blocks, arrived)

    @pl.when(parity_ref[0] == backward)
    def _():
        finish_backward(arrived, arrived_other, core_ref, *ins, *outs[1:], *scratch)

    @pl.when(parity_ref[0] != backward)
    def _():
        finish_forward(arrived, core_ref, reads_ref, *ins[:6], outs[0], scratch[0], scratch[3])


def add_rows(arrived, owned, core, half, rows_ref, added_of):
    blocks, refs = arrived
    for block in blocks:
        if block.owned == owned:
            columns = columns_of(core, block, half)
            rows_ref[rows_of(block), columns] = (
                part_of(block, refs).astype(jnp.float32) + added_of(block, columns)
            ).astype(jnp.bfloat16)


def half_copy(core, owned, half, rows_ref, target_ref, sem):
    owner = core if owned else 1 - core
    columns = pl.ds(pl.multiple_of(owner * half, half), half)
    return pltpu.make_async_copy(rows_ref.at[:, columns], target_ref.at[:, columns], sem)


def finish_forward(
    arrived,
    core_ref,
    reads_ref,
    part_ref,
    shared_other_ref,
    local_ref,
    shared_ref,
    proj_mine_ref,
    proj_other_ref,
    next_acts_ref,
    rows_ref,
    sems,
):
    half = proj_mine_ref.shape[1]
    core = core_ref[0]
    own = part_ref[:BLK, :BLK]
    near = jnp.exp(dot_nt(local_ref[...], shared_other_ref[:, :HS]) * SCALE)
    near = jnp.where(reads_ref[:1] > 0.0, near, 0.0)
    denominator = jnp.sum(own, axis=-1, keepdims=True) + jnp.sum(near, axis=-1, keepdims=True)
    attended = (
        dot_nn((own / denominator).astype(jnp.bfloat16), shared_ref[:, HS:])
        + dot_nn((near / denominator).astype(jnp.bfloat16), shared_other_ref[:, HS:])
    ).astype(jnp.bfloat16)

    def added_of(block, columns):
        return dot_nn(
            attended[block.row : block.row + block.size],
            weights_of(block, proj_mine_ref, proj_other_ref),
        )

    copies = []
    for index, owned in enumerate((False, True)):
        add_rows(arrived, owned, core, half, rows_ref, added_of)
        copies.append(half_copy(core, owned, half, rows_ref, next_acts_ref, sems.at[index]))
        copies[-1].start()
    for copy in copies:
        copy.wait()


def finish_backward(
    arrived,
    arrived_other,
    core_ref,
    part_ref,
    shared_other_ref,
    local_ref,
    shared_ref,
    proj_mine_ref,
    proj_other_ref,
    part_proj_ref,
    qkv_mine_ref,
    qkv_other_ref,
    stashed_ref,
    attended_ref,
    normed_ref,
    wide_ref,
    inverse_ref,
    soft_ref,
    turned_ref,
    wide_attended_ref,
    values_ref,
    keys_ref,
    queries_ref,
    next_grads_ref,
    grad_qkv_ref,
    grad_proj_ref,
    rows_ref,
    qkv_ref,
    proj_ref,
    sems,
):
    half = qkv_mine_ref.shape[1]
    core = core_ref[0]
    refs = (soft_ref, turned_ref, wide_attended_ref, values_ref, keys_ref, queries_ref)
    both, alone = back_through(1, shared_other_ref[:, :HS], refs)
    dprojected = jnp.concatenate(
        [part_ref[:BLK] + both[:BLK], part_ref[BLK:] + both[BLK:] + alone], axis=0
    ).astype(jnp.bfloat16)
    own = dprojected[:BLK]
    mean_term = jnp.sum(own.astype(jnp.float32) * wide_ref[...], axis=-1, keepdims=True)
    mean_term = mean_term / (2 * half)
    inverse = inverse_ref[...]
    pull = inverse * inverse * mean_term

    def added_of(block, columns):
        rows = rows_of(block)
        mine = slice(block.row, block.row + block.size)
        dnormed = dot_nn(own[mine], weights_of(block, qkv_mine_ref, qkv_other_ref))
        widened = stashed_ref[rows, columns].astype(jnp.float32)
        return inverse[mine] * dnormed - pull[mine] * widened

    copies = []
    add_rows(arrived, True, core, half, rows_ref, added_of)
    copies.append(half_copy(core, True, half, rows_ref, next_grads_ref, sems.at[2]))
    copies[-1].start()
    qkv_ref[...] = dot_tn(dprojected, normed_ref[...]).astype(jnp.bfloat16)
    copies.append(pltpu.make_async_copy(qkv_ref, grad_qkv_ref, sems.at[1]))
    copies[-1].start()
    add_rows(arrived, False, core, half, rows_ref, added_of)
    width = half // len(arrived_other)
    for index, other_ref in enumerate(arrived_other):
        columns = slice(index * width, (index + 1) * width)
        proj_ref[:, columns] = (
            part_proj_ref[:, columns] + other_ref[...].astype(jnp.float32)
        ).astype(jnp.bfloat16)
    copies.append(half_copy(core, False, half, rows_ref, next_grads_ref, sems.at[3]))
    copies[-1].start()
    copies.append(pltpu.make_async_copy(proj_ref, grad_proj_ref, sems.at[0]))
    copies[-1].start()
    for copy in copies:
        copy.wait()


def on_device(kernel, scalars, values, outputs, name):
    return pl.pallas_call(
        kernel,
        out_shape=[pltpu.VMEM(shape, dtype) for shape, dtype in outputs],
        in_specs=[pl.BlockSpec(memory_space=pltpu.SMEM)] * len(scalars)
        + [pl.BlockSpec(memory_space=pltpu.VMEM)] * len(values),
        out_specs=[pl.BlockSpec(memory_space=pltpu.VMEM)] * len(outputs),
        compiler_params=pltpu.CompilerParams(vmem_limit_bytes=VMEM_LIMIT),
        cost_estimate=COST,
        name=name,
    )(*scalars, *in_vmem(values))


def per_device(sent_acts, sent_grads, stashed, w_qkv, w_proj, neighbour):
    bf16, f32 = jnp.bfloat16, jnp.float32
    rows, features = stashed.shape
    half = features // 2
    core = lax.axis_index("shard").astype(jnp.int32).reshape(1)
    parity = (lax.axis_index("section").astype(jnp.int32) & 1).reshape(1)
    rest = LAST
    near_blocks = [
        Block(0, rows, False, 0, half, 0, 0),
        Block(0, rows, True, 0, half - rest, 0, half),
        Block(0, rows, True, half - rest, rest, 1, 0),
    ]
    size = rows // 2
    far_blocks = [
        Block(piece * size, size, owned, 0, half, piece, half * owned)
        for piece in range(2)
        for owned in (False, True)
    ]
    near_pieces = picked(near_blocks, (core, parity), sent_acts, sent_grads)
    near = [passed_on(piece, True) for piece in near_pieces]
    far_parity, _ = lax.optimization_barrier((parity, near_pieces[0]))
    far_pieces = picked(far_blocks, (core, far_parity), sent_grads, sent_acts)
    far = [passed_on(piece, False) for piece in far_pieces]
    qkv_mine = w_qkv[0].T
    proj_mine, neighbour, _ = lax.optimization_barrier(
        (w_proj[0], neighbour, near_pieces[0])
    )
    stashed, _ = lax.optimization_barrier((stashed, far_pieces[0]))
    normed_mine, normed_others, inverse, stashed = on_device(
        normed_kernel,
        (core,),
        (stashed,),
        [
            ((rows, half), bf16),
            ((rows, half), bf16),
            ((rows, 1), f32),
            ((rows, features), bf16),
        ],
        "norm",
    )
    normed_other, qkv_other = swapped(normed_others), swapped(qkv_mine)
    proj_other, near_other = swapped(proj_mine), swapped(neighbour)
    near_own = swapped(near_other)
    projected, wide, qkv_mine, proj_mine = on_device(
        project_kernel,
        (),
        (normed_mine, normed_others, qkv_mine, qkv_other, proj_mine),
        [
            ((rows, 3 * HS), bf16),
            ((rows, 3 * HS), f32),
            ((3 * HS, half), bf16),
            ((HS, half), bf16),
        ],
        "project",
    )
    soft, attended, reads, normed, *padded = on_device(
        attend_kernel,
        (core, near_own, near_other),
        (projected, swapped(projected), normed_mine, normed_other),
        [
            ((2 * rows, 2 * rows), f32),
            ((2 * rows, HS), bf16),
            ((8, rows), f32),
            ((2 * rows, half), bf16),
            ((2 * rows, 2 * rows), bf16),
            ((2 * rows, HS), f32),
            ((2 * rows, HS), bf16),
            ((2 * rows, 3 * HS), bf16),
            ((2 * rows, 3 * HS), bf16),
        ],
        "attend",
    )
    results, ready = (), soft
    weights = (qkv_mine, qkv_other, proj_mine, proj_other, attended)
    parts = [((HS, half // 2), bf16)] * 2
    given = [((rows, HS), bf16), ((rows, 2 * HS), bf16)]
    for backward, blocks, arrived in ((1, far_blocks, far), (0, near_blocks, near)):
        count = len(arrived)
        if backward:
            *arrived, ready = lax.optimization_barrier((*arrived, ready))
            local, shared, *others = on_device(
                functools.partial(arrive_kernel, backward, blocks, count, False, True),
                (parity,),
                (*arrived, *weights),
                given + parts,
                "arrive",
            )
            others = [swapped(piece) for piece in others]
        else:
            early, last = arrived
            early, ready = lax.optimization_barrier((early, ready))
            sums, squares, *others = on_device(
                functools.partial(arrive_kernel, backward, blocks[:-1], 1, False, False),
                (parity,),
                (early, *weights),
                [((rows, 3 * HS), f32), ((rows, 1), f32)] + parts,
                "begin",
            )
            others = [swapped(piece) for piece in others]
            last_block = [blocks[-1]._replace(array=0)]
            last, sums = lax.optimization_barrier((last, sums))
            local, shared = on_device(
                functools.partial(arrive_kernel, backward, last_block, 1, True, True),
                (parity,),
                (last, *weights, sums, squares),
                given,
                "arrive",
            )
            arrived = [early, last]
        shared_other = swapped(shared)
        part, part_proj = on_device(
            functools.partial(own_kernel, backward, blocks, count),
            (parity,),
            (*arrived, local, shared, attended, soft, *padded),
            [((2 * rows, 3 * HS), f32), ((HS, half), f32)],
            "own",
        )
        inputs = (
            *arrived,
            *others,
            reads,
            part,
            shared_other,
            local,
            shared,
            proj_mine,
            proj_other,
            part_proj,
            qkv_mine,
            qkv_other,
            stashed,
            attended,
            normed,
            wide,
            inverse,
            soft,
            *padded,
        )
        results = pl.pallas_call(
            functools.partial(
                finish_kernel, backward, blocks, count, len(others), len(results)
            ),
            out_shape=[
                jax.ShapeDtypeStruct(shape, bf16)
                for shape in ((rows, features), (rows, features), (3 * HS, half), (HS, half))
            ],
            in_specs=[pl.BlockSpec(memory_space=pltpu.SMEM)] * 2
            + [pl.BlockSpec(memory_space=pltpu.VMEM)] * len(inputs)
            + [pl.BlockSpec(memory_space=pl.ANY)] * len(results),
            out_specs=[pl.BlockSpec(memory_space=pl.ANY)] * 4,
            scratch_shapes=[
                pltpu.VMEM((rows, features), bf16),
                pltpu.VMEM((3 * HS, half), bf16),
                pltpu.VMEM((HS, half), bf16),
                pltpu.SemaphoreType.DMA((4,)),
            ],
            input_output_aliases={
                2 + len(inputs) + index: index for index in range(len(results))
            },
            compiler_params=pltpu.CompilerParams(vmem_limit_bytes=VMEM_LIMIT),
            cost_estimate=COST,
            name="finish",
        )(core, parity, *in_vmem(inputs), *results)
        ready = results[0]
    next_acts, next_grads, grad_qkv, grad_proj = results
    return (next_acts, next_grads, grad_qkv.T[None], grad_proj[None])


def solution(mesh):
    return jax.shard_map(
        per_device,
        mesh=mesh,
        in_specs=(
            P(("groups", "section", "shard"), None),
            P(("groups", "section", "shard"), None),
            P(("groups", "section", "shard"), None),
            P("section", "shard", None),
            P("section", None, "shard"),
            P(("groups", "section", "shard")),
        ),
        out_specs=(
            P(("groups", "section", "shard"), None),
            P(("groups", "section", "shard"), None),
            P(("groups", "section"), "shard", None),
            P(("groups", "section"), None, "shard"),
        ),
        check_vma=False,
    )
```

```python
import collections
import functools

import jax
import jax.numpy as jnp
from jax import lax
from jax.experimental import pallas as pl
from jax.experimental.pallas import tpu as pltpu
from jax.sharding import PartitionSpec as P

Block = collections.namedtuple(
    "Block", ["row", "size", "owned", "first", "width", "array", "at"]
)

HS = 64
BLK = 128
EPSILON = 1e-05
SCALE = HS**-0.5
VMEM_LIMIT = 16 * 1024 * 1024
LAST = 256
COST = pl.CostEstimate(flops=1024, bytes_accessed=4 * 1024 * 1024, transcendentals=0)


def passed_on(value, near):
    count = lax.axis_size("section")
    steps = (1, -1) if near else (-1, 1)
    pairs = [(source, (source + steps[source % 2]) % count) for source in range(count)]
    return lax.ppermute(value, "section", pairs)


def swapped(value):
    count = lax.axis_size("shard")
    return lax.ppermute(value, "shard", [(core, (core + 1) % count) for core in range(count)])


def dot_nn(first_op, second_op):
    return jnp.dot(first_op, second_op, preferred_element_type=jnp.float32)


def dot_nt(first_op, second_op):
    return lax.dot_general(
        first_op, second_op, (((1,), (1,)), ((), ())), preferred_element_type=jnp.float32
    )


def dot_tn(first_op, second_op):
    return lax.dot_general(
        first_op, second_op, (((0,), (0,)), ((), ())), preferred_element_type=jnp.float32
    )


def columns_of(core, block, half):
    owner = core if block.owned else 1 - core
    return pl.ds(pl.multiple_of(owner * half + block.first, 128), block.width)


def rows_of(block):
    return pl.ds(block.row, block.size)


def part_of(block, refs):
    return refs[block.array][:, block.at : block.at + block.width]


def weights_of(block, mine_ref, other_ref):
    return (mine_ref if block.owned else other_ref)[:, block.first : block.first + block.width]


def in_vmem(values):
    return [pltpu.with_memory_space_constraint(value, pltpu.VMEM) for value in values]


def in_hbm(values):
    return [pltpu.with_memory_space_constraint(value, pltpu.HBM) for value in values]


def pick_kernel(blocks, core_ref, parity_ref, even_rows_ref, odd_rows_ref, *refs):
    *outs, sems = refs
    half = even_rows_ref.shape[1] // 2

    def copy_from(source_ref):
        copies = []
        for index, block in enumerate(blocks):
            copies.append(
                pltpu.make_async_copy(
                    source_ref.at[rows_of(block), columns_of(core_ref[0], block, half)],
                    outs[block.array].at[:, block.at : block.at + block.width],
                    sems.at[index],
                )
            )
            copies[-1].start()
        for copy in copies:
            copy.wait()

    @pl.when(parity_ref[0] == 0)
    def _():
        copy_from(even_rows_ref)

    @pl.when(parity_ref[0] == 1)
    def _():
        copy_from(odd_rows_ref)


def picked(blocks, scalars, even_rows, odd_rows):
    shapes = {}
    for block in blocks:
        rows, columns = shapes.get(block.array, (0, 0))
        shapes[block.array] = (max(rows, block.size), max(columns, block.at + block.width))
    return pl.pallas_call(
        functools.partial(pick_kernel, blocks),
        out_shape=[pltpu.VMEM(shapes[array], even_rows.dtype) for array in sorted(shapes)],
        in_specs=[pl.BlockSpec(memory_space=pltpu.SMEM)] * 2
        + [pl.BlockSpec(memory_space=pl.ANY)] * 2,
        out_specs=[pl.BlockSpec(memory_space=pltpu.VMEM)] * len(shapes),
        scratch_shapes=[pltpu.SemaphoreType.DMA((len(blocks),))],
        compiler_params=pltpu.CompilerParams(vmem_limit_bytes=VMEM_LIMIT),
        cost_estimate=COST,
        name="pick",
    )(*scalars, *in_hbm((even_rows, odd_rows)))


def normed_kernel(
    core_ref, rows_ref, mine_ref, others_ref, inverse_ref, kept_ref
):
    kept_ref[...] = rows_ref[...]
    half = mine_ref.shape[1]
    widened = rows_ref[...].astype(jnp.float32)
    inverse = lax.rsqrt(jnp.mean(widened * widened, axis=-1, keepdims=True) + EPSILON)
    inverse_ref[...] = inverse
    for owner, half_ref in ((core_ref[0], mine_ref), (1 - core_ref[0], others_ref)):
        columns = pl.ds(pl.multiple_of(owner * half, half), half)
        half_ref[...] = (rows_ref[:, columns].astype(jnp.float32) * inverse).astype(jnp.bfloat16)


def project_kernel(
    mine_ref,
    others_ref,
    qkv_mine_ref,
    qkv_other_ref,
    proj_mine_ref,
    projected_ref,
    wide_ref,
    kept_qkv_ref,
    kept_proj_ref,
):
    kept_qkv_ref[...] = qkv_mine_ref[...]
    kept_proj_ref[...] = proj_mine_ref[...]
    projected = dot_nt(mine_ref[...], qkv_mine_ref[...]) + dot_nt(
        others_ref[...], qkv_other_ref[...]
    )
    wide_ref[...] = projected
    projected_ref[...] = projected.astype(jnp.bfloat16)


def attend_kernel(
    core_ref,
    near_ref,
    near_other_ref,
    own_ref,
    other_ref,
    normed_own_ref,
    normed_other_ref,
    soft_ref,
    attended_ref,
    reads_ref,
    normed_ref,
    turned_ref,
    wide_ref,
    values_ref,
    keys_ref,
    queries_ref,
):
    normed_ref[:BLK] = normed_own_ref[...]
    normed_ref[BLK:] = normed_other_ref[...]
    keys_ref[...] = jnp.zeros_like(keys_ref)
    queries_ref[...] = jnp.zeros_like(queries_ref)
    for index, projected_ref in enumerate((own_ref, other_ref)):
        rows = pl.ds(index * BLK, BLK)
        keys_ref[rows, :HS] = projected_ref[:, HS : 2 * HS]
        queries_ref[rows, HS : 2 * HS] = projected_ref[:, :HS]
        values_ref[rows, :] = projected_ref[:, 2 * HS :]
    core = core_ref[0]
    reads_ref[...] = jnp.full(reads_ref.shape, (near_ref[0] != core).astype(jnp.float32))
    keys = keys_ref[:, :HS]
    for index, (projected_ref, reads_both) in enumerate(
        ((own_ref, near_ref[0] != core), (other_ref, near_other_ref[0] != 1 - core))
    ):
        rows = pl.ds(index * BLK, BLK)
        scores = dot_nt(projected_ref[:, :HS], keys) * SCALE
        column = lax.broadcasted_iota(jnp.int32, scores.shape, 1)
        own_block = (column >= index * BLK) & (column < (index + 1) * BLK)
        exponent = jnp.where(own_block | reads_both, jnp.exp(scores), 0.0)
        soft = exponent / jnp.sum(exponent, axis=-1, keepdims=True)
        soft_ref[rows, :] = soft
        turned_ref[:, rows] = soft.T.astype(jnp.bfloat16)
        rounded = soft.astype(jnp.bfloat16)
        attended = dot_nn(rounded, values_ref[...])
        attended_ref[rows, :] = attended.astype(jnp.bfloat16)
        rest = (soft - rounded.astype(jnp.float32)).astype(jnp.bfloat16)
        wide_ref[rows, :] = attended + dot_nn(rest, values_ref[...])


def arrive_kernel(backward, blocks, forward_blocks, count, begun, ended, parity_ref, *refs):
    arrived, refs = refs[:count], refs[count:]
    qkv_mine_ref, qkv_other_ref, proj_mine_ref, proj_other_ref, attended_ref, *refs = refs
    if begun:
        sums_in_ref, *refs = refs
    if ended:
        local_ref, shared_ref, *part_refs = refs
    else:
        sums_out_ref, *part_refs = refs
    row_groups = sorted({(block.row, block.size) for block in blocks})

    def summed(some_blocks, term):
        sums = {}
        for block in some_blocks:
            part = term(block)
            sums[block.row] = sums[block.row] + part if block.row in sums else part
        return sums

    @pl.when(parity_ref[0] == backward)
    def _():
        if part_refs:
            part = sum(
                dot_tn(attended_ref[rows_of(block), :], part_of(block, arrived))
                for block in blocks
                if not block.owned
            ).astype(jnp.bfloat16)
            width = part_refs[0].shape[1]
            for index, part_ref in enumerate(part_refs):
                part_ref[...] = part[:, index * width : (index + 1) * width]

        def term(block):
            return dot_nt(part_of(block, arrived), weights_of(block, proj_mine_ref, proj_other_ref))

        sums = summed(blocks, term)
        for row, size in row_groups:
            rows = pl.ds(row, size)
            if begun:
                sums[row] += sums_in_ref[rows, :]
            if not ended:
                sums_out_ref[rows, :] = sums[row]
                continue
            grad_attended = sums[row].astype(jnp.bfloat16)
            local_ref[rows, :] = grad_attended
            shared_ref[rows, :HS] = grad_attended
            shared_ref[rows, HS:] = grad_attended

    @pl.when(parity_ref[0] != backward)
    def _():
        for part_ref in part_refs:
            part_ref[...] = jnp.zeros_like(part_ref)
        if not ended:
            sums_out_ref[...] = jnp.zeros_like(sums_out_ref)
            return

        def square(block):
            widened = part_of(block, arrived).astype(jnp.float32)
            return jnp.sum(widened * widened, axis=-1, keepdims=True)

        features = 2 * qkv_mine_ref.shape[1]
        squares = summed(forward_blocks, square)
        inverse = {row: lax.rsqrt(squares[row] / features + EPSILON) for row, _ in row_groups}

        def term(block):
            widened = part_of(block, arrived).astype(jnp.float32)
            normed = (widened * inverse[block.row]).astype(jnp.bfloat16)
            return dot_nt(normed, weights_of(block, qkv_mine_ref, qkv_other_ref))

        sums = summed(forward_blocks, term)
        for row, size in row_groups:
            projected = sums[row].astype(jnp.bfloat16)
            local_ref[pl.ds(row, size), :] = projected[:, :HS]
            shared_ref[pl.ds(row, size), :] = projected[:, HS:]


def own_kernel(backward, blocks, count, parity_ref, *refs):
    arrived, refs = refs[:count], refs[count:]
    local_ref, shared_ref, attended_ref, *refs = refs
    padded_refs, (part_ref, proj_ref) = refs[:6], refs[6:]

    @pl.when(parity_ref[0] == backward)
    def _():
        both, alone = back_through(0, local_ref[...], padded_refs)
        part_ref[:BLK] = both[:BLK] + alone
        part_ref[BLK:] = both[BLK:]
        sums = {}
        for block in blocks:
            if block.owned:
                term = dot_tn(attended_ref[rows_of(block), :], part_of(block, arrived))
                key = (block.first, block.width)
                sums[key] = sums[key] + term if key in sums else term
        for (first, width), total in sums.items():
            proj_ref[:, first : first + width] = total

    @pl.when(parity_ref[0] != backward)
    def _():
        part_ref[:BLK, :BLK] = jnp.exp(dot_nt(local_ref[...], shared_ref[:, :HS]) * SCALE)


def back_through(index, grad_attended, refs):
    soft_ref, turned_ref, wide_ref, values_ref, keys_ref, queries_ref = refs
    first = index * BLK
    soft = soft_ref[first : first + BLK]
    slope = dot_nt(grad_attended, values_ref[...])
    shared = jnp.sum(
        grad_attended.astype(jnp.float32) * wide_ref[first : first + BLK], axis=-1, keepdims=True
    )
    dscore = (soft * (slope - shared) * SCALE).astype(jnp.bfloat16)
    padded = jnp.concatenate([jnp.zeros((BLK, 2 * HS), jnp.bfloat16), grad_attended], axis=1)
    both = dot_tn(dscore, queries_ref[first : first + BLK]) + dot_nn(
        turned_ref[:, first : first + BLK], padded
    )
    return both, dot_nn(dscore, keys_ref[...])


def finish_kernel(backward, blocks, count, others, aliased, core_ref, parity_ref, *refs):
    arrived, refs = refs[:count], refs[count:]
    arrived_other, refs = refs[:others], refs[others:]
    reads_ref, *refs = refs
    ins, outs, scratch = refs[:20], refs[20 + aliased : 24 + aliased], refs[24 + aliased :]
    arrived = (blocks, arrived)

    @pl.when(parity_ref[0] == backward)
    def _():
        finish_backward(arrived, arrived_other, core_ref, *ins, *outs[1:], *scratch)

    @pl.when(parity_ref[0] != backward)
    def _():
        finish_forward(arrived, core_ref, reads_ref, *ins[:6], outs[0], scratch[0], scratch[3])


def add_rows(arrived, owned, core, half, rows_ref, added_of):
    blocks, refs = arrived
    for block in blocks:
        if block.owned == owned:
            columns = columns_of(core, block, half)
            rows_ref[rows_of(block), columns] = (
                part_of(block, refs).astype(jnp.float32) + added_of(block, columns)
            ).astype(jnp.bfloat16)


def half_copy(core, owned, half, rows_ref, target_ref, sem):
    owner = core if owned else 1 - core
    columns = pl.ds(pl.multiple_of(owner * half, half), half)
    return pltpu.make_async_copy(rows_ref.at[:, columns], target_ref.at[:, columns], sem)


def finish_forward(
    arrived,
    core_ref,
    reads_ref,
    part_ref,
    shared_other_ref,
    local_ref,
    shared_ref,
    proj_mine_ref,
    proj_other_ref,
    next_acts_ref,
    rows_ref,
    sems,
):
    half = proj_mine_ref.shape[1]
    core = core_ref[0]
    own = part_ref[:BLK, :BLK]
    near = jnp.exp(dot_nt(local_ref[...], shared_other_ref[:, :HS]) * SCALE)
    near = jnp.where(reads_ref[:1] > 0.0, near, 0.0)
    denominator = jnp.sum(own, axis=-1, keepdims=True) + jnp.sum(near, axis=-1, keepdims=True)
    attended = (
        dot_nn((own / denominator).astype(jnp.bfloat16), shared_ref[:, HS:])
        + dot_nn((near / denominator).astype(jnp.bfloat16), shared_other_ref[:, HS:])
    ).astype(jnp.bfloat16)

    def added_of(block, columns):
        return dot_nn(
            attended[block.row : block.row + block.size],
            weights_of(block, proj_mine_ref, proj_other_ref),
        )

    copies = []
    for index, owned in enumerate((False, True)):
        add_rows(arrived, owned, core, half, rows_ref, added_of)
        copies.append(half_copy(core, owned, half, rows_ref, next_acts_ref, sems.at[index]))
        copies[-1].start()
    for copy in copies:
        copy.wait()


def finish_backward(
    arrived,
    arrived_other,
    core_ref,
    part_ref,
    shared_other_ref,
    local_ref,
    shared_ref,
    proj_mine_ref,
    proj_other_ref,
    part_proj_ref,
    qkv_mine_ref,
    qkv_other_ref,
    stashed_ref,
    attended_ref,
    normed_ref,
    wide_ref,
    inverse_ref,
    soft_ref,
    turned_ref,
    wide_attended_ref,
    values_ref,
    keys_ref,
    queries_ref,
    next_grads_ref,
    grad_qkv_ref,
    grad_proj_ref,
    rows_ref,
    qkv_ref,
    proj_ref,
    sems,
):
    half = qkv_mine_ref.shape[1]
    core = core_ref[0]
    refs = (soft_ref, turned_ref, wide_attended_ref, values_ref, keys_ref, queries_ref)
    both, alone = back_through(1, shared_other_ref[:, :HS], refs)
    dprojected = jnp.concatenate(
        [part_ref[:BLK] + both[:BLK], part_ref[BLK:] + both[BLK:] + alone], axis=0
    ).astype(jnp.bfloat16)
    own = dprojected[:BLK]
    mean_term = jnp.sum(own.astype(jnp.float32) * wide_ref[...], axis=-1, keepdims=True)
    mean_term = mean_term / (2 * half)
    inverse = inverse_ref[...]
    pull = inverse * inverse * mean_term

    def added_of(block, columns):
        rows = rows_of(block)
        mine = slice(block.row, block.row + block.size)
        dnormed = dot_nn(own[mine], weights_of(block, qkv_mine_ref, qkv_other_ref))
        widened = stashed_ref[rows, columns].astype(jnp.float32)
        return inverse[mine] * dnormed - pull[mine] * widened

    copies = []
    add_rows(arrived, True, core, half, rows_ref, added_of)
    copies.append(half_copy(core, True, half, rows_ref, next_grads_ref, sems.at[2]))
    copies[-1].start()
    qkv_ref[...] = dot_tn(dprojected, normed_ref[...]).astype(jnp.bfloat16)
    copies.append(pltpu.make_async_copy(qkv_ref, grad_qkv_ref, sems.at[1]))
    copies[-1].start()
    add_rows(arrived, False, core, half, rows_ref, added_of)
    width = half // len(arrived_other)
    for index, other_ref in enumerate(arrived_other):
        columns = slice(index * width, (index + 1) * width)
        proj_ref[:, columns] = (
            part_proj_ref[:, columns] + other_ref[...].astype(jnp.float32)
        ).astype(jnp.bfloat16)
    copies.append(half_copy(core, False, half, rows_ref, next_grads_ref, sems.at[3]))
    copies[-1].start()
    copies.append(pltpu.make_async_copy(proj_ref, grad_proj_ref, sems.at[0]))
    copies[-1].start()
    for copy in copies:
        copy.wait()


def on_device(kernel, scalars, values, outputs, name):
    return pl.pallas_call(
        kernel,
        out_shape=[pltpu.VMEM(shape, dtype) for shape, dtype in outputs],
        in_specs=[pl.BlockSpec(memory_space=pltpu.SMEM)] * len(scalars)
        + [pl.BlockSpec(memory_space=pltpu.VMEM)] * len(values),
        out_specs=[pl.BlockSpec(memory_space=pltpu.VMEM)] * len(outputs),
        compiler_params=pltpu.CompilerParams(vmem_limit_bytes=VMEM_LIMIT),
        cost_estimate=COST,
        name=name,
    )(*scalars, *in_vmem(values))


def per_device(sent_acts, sent_grads, stashed, w_qkv, w_proj, neighbour):
    bf16, f32 = jnp.bfloat16, jnp.float32
    rows, features = stashed.shape
    half = features // 2
    core = lax.axis_index("shard").astype(jnp.int32).reshape(1)
    parity = (lax.axis_index("section").astype(jnp.int32) & 1).reshape(1)
    rest = LAST
    near_blocks = [
        Block(0, rows, False, 0, half, 0, 0),
        Block(0, rows, True, 0, half - rest, 0, half),
        Block(0, rows, True, half - rest, rest, 1, 0),
    ]
    size = rows // 2
    far_blocks = [
        Block(piece * size, size, owned, 0, half, piece, half * owned)
        for piece in range(2)
        for owned in (False, True)
    ]
    near_pieces = picked(near_blocks, (core, parity), sent_acts, sent_grads)
    near = [passed_on(piece, True) for piece in near_pieces]
    far_parity, _ = lax.optimization_barrier((parity, near_pieces[0]))
    far_pieces = picked(far_blocks, (core, far_parity), sent_grads, sent_acts)
    far = [passed_on(piece, False) for piece in far_pieces]
    qkv_mine = w_qkv[0].T
    proj_mine, neighbour, _ = lax.optimization_barrier(
        (w_proj[0], neighbour, near_pieces[0])
    )
    stashed, _ = lax.optimization_barrier((stashed, far_pieces[0]))
    normed_mine, normed_others, inverse, stashed = on_device(
        normed_kernel,
        (core,),
        (stashed,),
        [
            ((rows, half), bf16),
            ((rows, half), bf16),
            ((rows, 1), f32),
            ((rows, features), bf16),
        ],
        "norm",
    )
    normed_other, qkv_other = swapped(normed_others), swapped(qkv_mine)
    proj_other, near_other = swapped(proj_mine), swapped(neighbour)
    near_own = swapped(near_other)
    projected, wide, qkv_mine, proj_mine = on_device(
        project_kernel,
        (),
        (normed_mine, normed_others, qkv_mine, qkv_other, proj_mine),
        [
            ((rows, 3 * HS), bf16),
            ((rows, 3 * HS), f32),
            ((3 * HS, half), bf16),
            ((HS, half), bf16),
        ],
        "project",
    )
    soft, attended, reads, normed, *padded = on_device(
        attend_kernel,
        (core, near_own, near_other),
        (projected, swapped(projected), normed_mine, normed_other),
        [
            ((2 * rows, 2 * rows), f32),
            ((2 * rows, HS), bf16),
            ((8, rows), f32),
            ((2 * rows, half), bf16),
            ((2 * rows, 2 * rows), bf16),
            ((2 * rows, HS), f32),
            ((2 * rows, HS), bf16),
            ((2 * rows, 3 * HS), bf16),
            ((2 * rows, 3 * HS), bf16),
        ],
        "attend",
    )
    results, ready = (), soft
    weights = (qkv_mine, qkv_other, proj_mine, proj_other, attended)
    parts = [((HS, half // 2), bf16)] * 2
    given = [((rows, HS), bf16), ((rows, 2 * HS), bf16)]
    for backward, blocks, arrived in ((1, far_blocks, far), (0, near_blocks, near)):
        count = len(arrived)
        if backward:
            *arrived, ready = lax.optimization_barrier((*arrived, ready))
            local, shared, *others = on_device(
                functools.partial(arrive_kernel, backward, blocks, blocks, count, False, True),
                (parity,),
                (*arrived, *weights),
                given + parts,
                "arrive",
            )
            others = [swapped(piece) for piece in others]
        else:
            early, last = arrived
            early, ready = lax.optimization_barrier((early, ready))
            sums, *others = on_device(
                functools.partial(
                    arrive_kernel, backward, blocks[:-1], (), 1, False, False
                ),
                (parity,),
                (early, *weights),
                [((rows, HS), f32)] + parts,
                "begin",
            )
            others = [swapped(piece) for piece in others]
            last, sums = lax.optimization_barrier((last, sums))
            local, shared = on_device(
                functools.partial(
                    arrive_kernel, backward, blocks[-1:], blocks, count, True, True
                ),
                (parity,),
                (early, last, *weights, sums),
                given,
                "arrive",
            )
            arrived = [early, last]
        shared_other = swapped(shared)
        part, part_proj = on_device(
            functools.partial(own_kernel, backward, blocks, count),
            (parity,),
            (*arrived, local, shared, attended, soft, *padded),
            [((2 * rows, 3 * HS), f32), ((HS, half), f32)],
            "own",
        )
        inputs = (
            *arrived,
            *others,
            reads,
            part,
            shared_other,
            local,
            shared,
            proj_mine,
            proj_other,
            part_proj,
            qkv_mine,
            qkv_other,
            stashed,
            attended,
            normed,
            wide,
            inverse,
            soft,
            *padded,
        )
        results = pl.pallas_call(
            functools.partial(
                finish_kernel, backward, blocks, count, len(others), len(results)
            ),
            out_shape=[
                jax.ShapeDtypeStruct(shape, bf16)
                for shape in ((rows, features), (rows, features), (3 * HS, half), (HS, half))
            ],
            in_specs=[pl.BlockSpec(memory_space=pltpu.SMEM)] * 2
            + [pl.BlockSpec(memory_space=pltpu.VMEM)] * len(inputs)
            + [pl.BlockSpec(memory_space=pl.ANY)] * len(results),
            out_specs=[pl.BlockSpec(memory_space=pl.ANY)] * 4,
            scratch_shapes=[
                pltpu.VMEM((rows, features), bf16),
                pltpu.VMEM((3 * HS, half), bf16),
                pltpu.VMEM((HS, half), bf16),
                pltpu.SemaphoreType.DMA((4,)),
            ],
            input_output_aliases={
                2 + len(inputs) + index: index for index in range(len(results))
            },
            compiler_params=pltpu.CompilerParams(vmem_limit_bytes=VMEM_LIMIT),
            cost_estimate=COST,
            name="finish",
        )(core, parity, *in_vmem(inputs), *results)
        ready = results[0]
    next_acts, next_grads, grad_qkv, grad_proj = results
    return (next_acts, next_grads, grad_qkv.T[None], grad_proj[None])


def solution(mesh):
    return jax.shard_map(
        per_device,
        mesh=mesh,
        in_specs=(
            P(("groups", "section", "shard"), None),
            P(("groups", "section", "shard"), None),
            P(("groups", "section", "shard"), None),
            P("section", "shard", None),
            P("section", None, "shard"),
            P(("groups", "section", "shard")),
        ),
        out_specs=(
            P(("groups", "section", "shard"), None),
            P(("groups", "section", "shard"), None),
            P(("groups", "section"), "shard", None),
            P(("groups", "section"), None, "shard"),
        ),
        check_vma=False,
    )
```

```python
import collections
import functools

import jax
import jax.numpy as jnp
from jax import lax
from jax.experimental import pallas as pl
from jax.experimental.pallas import tpu as pltpu
from jax.sharding import PartitionSpec as P

Block = collections.namedtuple(
    "Block", ["row", "size", "owned", "first", "width", "array", "at"]
)

HS = 64
BLK = 128
EPSILON = 1e-05
SCALE = HS**-0.5
VMEM_LIMIT = 16 * 1024 * 1024
LAST = 256
COST = pl.CostEstimate(flops=1024, bytes_accessed=4 * 1024 * 1024, transcendentals=0)


def passed_on(value, near):
    count = lax.axis_size("section")
    steps = (1, -1) if near else (-1, 1)
    pairs = [(source, (source + steps[source % 2]) % count) for source in range(count)]
    return lax.ppermute(value, "section", pairs)


def swapped(value):
    count = lax.axis_size("shard")
    return lax.ppermute(value, "shard", [(core, (core + 1) % count) for core in range(count)])


def dot_nn(first_op, second_op):
    return jnp.dot(first_op, second_op, preferred_element_type=jnp.float32)


def dot_nt(first_op, second_op):
    return lax.dot_general(
        first_op, second_op, (((1,), (1,)), ((), ())), preferred_element_type=jnp.float32
    )


def dot_tn(first_op, second_op):
    return lax.dot_general(
        first_op, second_op, (((0,), (0,)), ((), ())), preferred_element_type=jnp.float32
    )


def columns_of(core, block, half):
    owner = core if block.owned else 1 - core
    return pl.ds(pl.multiple_of(owner * half + block.first, 128), block.width)


def rows_of(block):
    return pl.ds(block.row, block.size)


def part_of(block, refs):
    return refs[block.array][:, block.at : block.at + block.width]


def weights_of(block, mine_ref, other_ref):
    return (mine_ref if block.owned else other_ref)[:, block.first : block.first + block.width]


def in_vmem(values):
    return [pltpu.with_memory_space_constraint(value, pltpu.VMEM) for value in values]


def in_hbm(values):
    return [pltpu.with_memory_space_constraint(value, pltpu.HBM) for value in values]


def pick_kernel(blocks, core_ref, parity_ref, even_rows_ref, odd_rows_ref, *refs):
    *outs, sems = refs
    half = even_rows_ref.shape[1] // 2

    def copy_from(source_ref):
        copies = []
        for index, block in enumerate(blocks):
            copies.append(
                pltpu.make_async_copy(
                    source_ref.at[rows_of(block), columns_of(core_ref[0], block, half)],
                    outs[block.array].at[:, block.at : block.at + block.width],
                    sems.at[index],
                )
            )
            copies[-1].start()
        for copy in copies:
            copy.wait()

    @pl.when(parity_ref[0] == 0)
    def _():
        copy_from(even_rows_ref)

    @pl.when(parity_ref[0] == 1)
    def _():
        copy_from(odd_rows_ref)


def picked(blocks, scalars, even_rows, odd_rows):
    shapes = {}
    for block in blocks:
        rows, columns = shapes.get(block.array, (0, 0))
        shapes[block.array] = (max(rows, block.size), max(columns, block.at + block.width))
    return pl.pallas_call(
        functools.partial(pick_kernel, blocks),
        out_shape=[pltpu.VMEM(shapes[array], even_rows.dtype) for array in sorted(shapes)],
        in_specs=[pl.BlockSpec(memory_space=pltpu.SMEM)] * 2
        + [pl.BlockSpec(memory_space=pl.ANY)] * 2,
        out_specs=[pl.BlockSpec(memory_space=pltpu.VMEM)] * len(shapes),
        scratch_shapes=[pltpu.SemaphoreType.DMA((len(blocks),))],
        compiler_params=pltpu.CompilerParams(vmem_limit_bytes=VMEM_LIMIT),
        cost_estimate=COST,
        name="pick",
    )(*scalars, *in_hbm((even_rows, odd_rows)))


def normed_kernel(
    core_ref, rows_ref, mine_ref, others_ref, inverse_ref, kept_ref
):
    kept_ref[...] = rows_ref[...]
    half = mine_ref.shape[1]
    widened = rows_ref[...].astype(jnp.float32)
    inverse = lax.rsqrt(jnp.mean(widened * widened, axis=-1, keepdims=True) + EPSILON)
    inverse_ref[...] = inverse
    for owner, half_ref in ((core_ref[0], mine_ref), (1 - core_ref[0], others_ref)):
        columns = pl.ds(pl.multiple_of(owner * half, half), half)
        half_ref[...] = (rows_ref[:, columns].astype(jnp.float32) * inverse).astype(jnp.bfloat16)


def project_kernel(
    mine_ref,
    others_ref,
    qkv_mine_ref,
    qkv_other_ref,
    proj_mine_ref,
    projected_ref,
    wide_ref,
    kept_qkv_ref,
    kept_proj_ref,
):
    kept_qkv_ref[...] = qkv_mine_ref[...]
    kept_proj_ref[...] = proj_mine_ref[...]
    projected = dot_nt(mine_ref[...], qkv_mine_ref[...]) + dot_nt(
        others_ref[...], qkv_other_ref[...]
    )
    wide_ref[...] = projected
    projected_ref[...] = projected.astype(jnp.bfloat16)


def attend_kernel(
    core_ref,
    near_ref,
    near_other_ref,
    own_ref,
    other_ref,
    normed_own_ref,
    normed_other_ref,
    soft_ref,
    attended_ref,
    reads_ref,
    normed_ref,
    turned_ref,
    wide_ref,
    values_ref,
    keys_ref,
    queries_ref,
):
    normed_ref[:BLK] = normed_own_ref[...]
    normed_ref[BLK:] = normed_other_ref[...]
    keys_ref[...] = jnp.zeros_like(keys_ref)
    queries_ref[...] = jnp.zeros_like(queries_ref)
    for index, projected_ref in enumerate((own_ref, other_ref)):
        rows = pl.ds(index * BLK, BLK)
        keys_ref[rows, :HS] = projected_ref[:, HS : 2 * HS]
        queries_ref[rows, HS : 2 * HS] = projected_ref[:, :HS]
        values_ref[rows, :] = projected_ref[:, 2 * HS :]
    core = core_ref[0]
    reads_ref[...] = jnp.full(reads_ref.shape, (near_ref[0] != core).astype(jnp.float32))
    keys = keys_ref[:, :HS]
    for index, (projected_ref, reads_both) in enumerate(
        ((own_ref, near_ref[0] != core), (other_ref, near_other_ref[0] != 1 - core))
    ):
        rows = pl.ds(index * BLK, BLK)
        scores = dot_nt(projected_ref[:, :HS], keys) * SCALE
        column = lax.broadcasted_iota(jnp.int32, scores.shape, 1)
        own_block = (column >= index * BLK) & (column < (index + 1) * BLK)
        exponent = jnp.where(own_block | reads_both, jnp.exp(scores), 0.0)
        soft = exponent / jnp.sum(exponent, axis=-1, keepdims=True)
        soft_ref[rows, :] = soft
        turned_ref[:, rows] = soft.T.astype(jnp.bfloat16)
        rounded = soft.astype(jnp.bfloat16)
        attended = dot_nn(rounded, values_ref[...])
        attended_ref[rows, :] = attended.astype(jnp.bfloat16)
        rest = (soft - rounded.astype(jnp.float32)).astype(jnp.bfloat16)
        wide_ref[rows, :] = attended + dot_nn(rest, values_ref[...])


def arrive_kernel(backward, blocks, forward_blocks, count, begun, ended, parity_ref, *refs):
    arrived, refs = refs[:count], refs[count:]
    qkv_mine_ref, qkv_other_ref, proj_mine_ref, proj_other_ref, attended_ref, *refs = refs
    if begun:
        sums_in_ref, *refs = refs
    if ended:
        local_ref, shared_ref, *part_refs = refs
    else:
        sums_out_ref, *part_refs = refs
    row_groups = sorted({(block.row, block.size) for block in blocks})

    def summed(some_blocks, term):
        sums = {}
        for block in some_blocks:
            part = term(block)
            sums[block.row] = sums[block.row] + part if block.row in sums else part
        return sums

    @pl.when(parity_ref[0] == backward)
    def _():
        if part_refs:
            part = sum(
                dot_tn(attended_ref[rows_of(block), :], part_of(block, arrived))
                for block in blocks
                if not block.owned
            ).astype(jnp.bfloat16)
            width = part_refs[0].shape[1]
            for index, part_ref in enumerate(part_refs):
                part_ref[...] = part[:, index * width : (index + 1) * width]

        def term(block):
            return dot_nt(part_of(block, arrived), weights_of(block, proj_mine_ref, proj_other_ref))

        sums = summed(blocks, term)
        for row, size in row_groups:
            rows = pl.ds(row, size)
            if begun:
                sums[row] += sums_in_ref[rows, :]
            if not ended:
                sums_out_ref[rows, :] = sums[row]
                continue
            grad_attended = sums[row].astype(jnp.bfloat16)
            local_ref[rows, :] = grad_attended
            shared_ref[rows, :HS] = grad_attended
            shared_ref[rows, HS:] = grad_attended

    @pl.when(parity_ref[0] != backward)
    def _():
        for part_ref in part_refs:
            part_ref[...] = jnp.zeros_like(part_ref)
        if not ended:
            sums_out_ref[...] = jnp.zeros_like(sums_out_ref)
            return

        def square(block):
            widened = part_of(block, arrived).astype(jnp.float32)
            return jnp.sum(widened * widened, axis=-1, keepdims=True)

        features = 2 * qkv_mine_ref.shape[1]
        squares = summed(forward_blocks, square)
        inverse = {row: lax.rsqrt(squares[row] / features + EPSILON) for row, _ in row_groups}

        def term(block):
            widened = part_of(block, arrived).astype(jnp.float32)
            normed = (widened * inverse[block.row]).astype(jnp.bfloat16)
            return dot_nt(normed, weights_of(block, qkv_mine_ref, qkv_other_ref))

        sums = summed(forward_blocks, term)
        for row, size in row_groups:
            projected = sums[row].astype(jnp.bfloat16)
            local_ref[pl.ds(row, size), :] = projected[:, :HS]
            shared_ref[pl.ds(row, size), :] = projected[:, HS:]


def own_kernel(backward, blocks, count, others, parity_ref, *refs):
    arrived, refs = refs[:count], refs[count:]
    arrived_other, refs = refs[:others], refs[others:]
    local_ref, shared_ref, attended_ref, *refs = refs
    padded_refs, (part_ref, proj_ref) = refs[:6], refs[6:]

    @pl.when(parity_ref[0] == backward)
    def _():
        both, alone = back_through(0, local_ref[...], padded_refs)
        part_ref[:BLK] = both[:BLK] + alone
        part_ref[BLK:] = both[BLK:]
        sums = {}
        for block in blocks:
            if block.owned:
                term = dot_tn(attended_ref[rows_of(block), :], part_of(block, arrived))
                key = (block.first, block.width)
                sums[key] = sums[key] + term if key in sums else term
        other = jnp.concatenate([other_ref[...] for other_ref in arrived_other], axis=1)
        for (first, width), total in sums.items():
            part = other[:, first : first + width].astype(jnp.float32)
            proj_ref[:, first : first + width] = (total + part).astype(jnp.bfloat16)

    @pl.when(parity_ref[0] != backward)
    def _():
        part_ref[:BLK, :BLK] = jnp.exp(dot_nt(local_ref[...], shared_ref[:, :HS]) * SCALE)


def back_through(index, grad_attended, refs):
    soft_ref, turned_ref, wide_ref, values_ref, keys_ref, queries_ref = refs
    first = index * BLK
    soft = soft_ref[first : first + BLK]
    slope = dot_nt(grad_attended, values_ref[...])
    shared = jnp.sum(
        grad_attended.astype(jnp.float32) * wide_ref[first : first + BLK], axis=-1, keepdims=True
    )
    dscore = (soft * (slope - shared) * SCALE).astype(jnp.bfloat16)
    padded = jnp.concatenate([jnp.zeros((BLK, 2 * HS), jnp.bfloat16), grad_attended], axis=1)
    both = dot_tn(dscore, queries_ref[first : first + BLK]) + dot_nn(
        turned_ref[:, first : first + BLK], padded
    )
    return both, dot_nn(dscore, keys_ref[...])


def finish_kernel(backward, blocks, count, aliased, core_ref, parity_ref, *refs):
    arrived, refs = refs[:count], refs[count:]
    reads_ref, *refs = refs
    ins, outs, scratch = refs[:20], refs[20 + aliased : 24 + aliased], refs[24 + aliased :]
    arrived = (blocks, arrived)

    @pl.when(parity_ref[0] == backward)
    def _():
        finish_backward(arrived, core_ref, *ins, *outs[1:], *scratch)

    @pl.when(parity_ref[0] != backward)
    def _():
        finish_forward(arrived, core_ref, reads_ref, *ins[:6], outs[0], scratch[0], scratch[2])


def add_rows(arrived, owned, core, half, rows_ref, added_of):
    blocks, refs = arrived
    for block in blocks:
        if block.owned == owned:
            columns = columns_of(core, block, half)
            rows_ref[rows_of(block), columns] = (
                part_of(block, refs).astype(jnp.float32) + added_of(block, columns)
            ).astype(jnp.bfloat16)


def half_copy(core, owned, half, rows_ref, target_ref, sem):
    owner = core if owned else 1 - core
    columns = pl.ds(pl.multiple_of(owner * half, half), half)
    return pltpu.make_async_copy(rows_ref.at[:, columns], target_ref.at[:, columns], sem)


def finish_forward(
    arrived,
    core_ref,
    reads_ref,
    part_ref,
    shared_other_ref,
    local_ref,
    shared_ref,
    proj_mine_ref,
    proj_other_ref,
    next_acts_ref,
    rows_ref,
    sems,
):
    half = proj_mine_ref.shape[1]
    core = core_ref[0]
    own = part_ref[:BLK, :BLK]
    near = jnp.exp(dot_nt(local_ref[...], shared_other_ref[:, :HS]) * SCALE)
    near = jnp.where(reads_ref[:1] > 0.0, near, 0.0)
    denominator = jnp.sum(own, axis=-1, keepdims=True) + jnp.sum(near, axis=-1, keepdims=True)
    attended = (
        dot_nn((own / denominator).astype(jnp.bfloat16), shared_ref[:, HS:])
        + dot_nn((near / denominator).astype(jnp.bfloat16), shared_other_ref[:, HS:])
    ).astype(jnp.bfloat16)

    def added_of(block, columns):
        return dot_nn(
            attended[block.row : block.row + block.size],
            weights_of(block, proj_mine_ref, proj_other_ref),
        )

    copies = []
    for index, owned in enumerate((False, True)):
        add_rows(arrived, owned, core, half, rows_ref, added_of)
        copies.append(half_copy(core, owned, half, rows_ref, next_acts_ref, sems.at[index]))
        copies[-1].start()
    for copy in copies:
        copy.wait()


def finish_backward(
    arrived,
    core_ref,
    part_ref,
    shared_other_ref,
    local_ref,
    shared_ref,
    proj_mine_ref,
    proj_other_ref,
    whole_proj_ref,
    qkv_mine_ref,
    qkv_other_ref,
    stashed_ref,
    attended_ref,
    normed_ref,
    wide_ref,
    inverse_ref,
    soft_ref,
    turned_ref,
    wide_attended_ref,
    values_ref,
    keys_ref,
    queries_ref,
    next_grads_ref,
    grad_qkv_ref,
    grad_proj_ref,
    rows_ref,
    qkv_ref,
    sems,
):
    copies = [pltpu.make_async_copy(whole_proj_ref, grad_proj_ref, sems.at[0])]
    copies[-1].start()
    half = qkv_mine_ref.shape[1]
    core = core_ref[0]
    refs = (soft_ref, turned_ref, wide_attended_ref, values_ref, keys_ref, queries_ref)
    both, alone = back_through(1, shared_other_ref[:, :HS], refs)
    dprojected = jnp.concatenate(
        [part_ref[:BLK] + both[:BLK], part_ref[BLK:] + both[BLK:] + alone], axis=0
    ).astype(jnp.bfloat16)
    own = dprojected[:BLK]
    mean_term = jnp.sum(own.astype(jnp.float32) * wide_ref[...], axis=-1, keepdims=True)
    mean_term = mean_term / (2 * half)
    inverse = inverse_ref[...]
    pull = inverse * inverse * mean_term

    def added_of(block, columns):
        rows = rows_of(block)
        mine = slice(block.row, block.row + block.size)
        dnormed = dot_nn(own[mine], weights_of(block, qkv_mine_ref, qkv_other_ref))
        widened = stashed_ref[rows, columns].astype(jnp.float32)
        return inverse[mine] * dnormed - pull[mine] * widened

    add_rows(arrived, True, core, half, rows_ref, added_of)
    copies.append(half_copy(core, True, half, rows_ref, next_grads_ref, sems.at[2]))
    copies[-1].start()
    qkv_ref[...] = dot_tn(dprojected, normed_ref[...]).astype(jnp.bfloat16)
    copies.append(pltpu.make_async_copy(qkv_ref, grad_qkv_ref, sems.at[1]))
    copies[-1].start()
    add_rows(arrived, False, core, half, rows_ref, added_of)
    copies.append(half_copy(core, False, half, rows_ref, next_grads_ref, sems.at[3]))
    copies[-1].start()
    for copy in copies:
        copy.wait()


def on_device(kernel, scalars, values, outputs, name):
    return pl.pallas_call(
        kernel,
        out_shape=[pltpu.VMEM(shape, dtype) for shape, dtype in outputs],
        in_specs=[pl.BlockSpec(memory_space=pltpu.SMEM)] * len(scalars)
        + [pl.BlockSpec(memory_space=pltpu.VMEM)] * len(values),
        out_specs=[pl.BlockSpec(memory_space=pltpu.VMEM)] * len(outputs),
        compiler_params=pltpu.CompilerParams(vmem_limit_bytes=VMEM_LIMIT),
        cost_estimate=COST,
        name=name,
    )(*scalars, *in_vmem(values))


def per_device(sent_acts, sent_grads, stashed, w_qkv, w_proj, neighbour):
    bf16, f32 = jnp.bfloat16, jnp.float32
    rows, features = stashed.shape
    half = features // 2
    core = lax.axis_index("shard").astype(jnp.int32).reshape(1)
    parity = (lax.axis_index("section").astype(jnp.int32) & 1).reshape(1)
    rest = LAST
    near_blocks = [
        Block(0, rows, False, 0, half, 0, 0),
        Block(0, rows, True, 0, half - rest, 0, half),
        Block(0, rows, True, half - rest, rest, 1, 0),
    ]
    size = rows // 2
    far_blocks = [
        Block(piece * size, size, owned, 0, half, piece, half * owned)
        for piece in range(2)
        for owned in (False, True)
    ]
    near_pieces = picked(near_blocks, (core, parity), sent_acts, sent_grads)
    near = [passed_on(piece, True) for piece in near_pieces]
    far_parity, _ = lax.optimization_barrier((parity, near_pieces[0]))
    far_pieces = picked(far_blocks, (core, far_parity), sent_grads, sent_acts)
    far = [passed_on(piece, False) for piece in far_pieces]
    qkv_mine = w_qkv[0].T
    proj_mine, neighbour, _ = lax.optimization_barrier(
        (w_proj[0], neighbour, near_pieces[0])
    )
    stashed, _ = lax.optimization_barrier((stashed, far_pieces[0]))
    normed_mine, normed_others, inverse, stashed = on_device(
        normed_kernel,
        (core,),
        (stashed,),
        [
            ((rows, half), bf16),
            ((rows, half), bf16),
            ((rows, 1), f32),
            ((rows, features), bf16),
        ],
        "norm",
    )
    normed_other, qkv_other = swapped(normed_others), swapped(qkv_mine)
    proj_other, near_other = swapped(proj_mine), swapped(neighbour)
    near_own = swapped(near_other)
    projected, wide, qkv_mine, proj_mine = on_device(
        project_kernel,
        (),
        (normed_mine, normed_others, qkv_mine, qkv_other, proj_mine),
        [
            ((rows, 3 * HS), bf16),
            ((rows, 3 * HS), f32),
            ((3 * HS, half), bf16),
            ((HS, half), bf16),
        ],
        "project",
    )
    soft, attended, reads, normed, *padded = on_device(
        attend_kernel,
        (core, near_own, near_other),
        (projected, swapped(projected), normed_mine, normed_other),
        [
            ((2 * rows, 2 * rows), f32),
            ((2 * rows, HS), bf16),
            ((8, rows), f32),
            ((2 * rows, half), bf16),
            ((2 * rows, 2 * rows), bf16),
            ((2 * rows, HS), f32),
            ((2 * rows, HS), bf16),
            ((2 * rows, 3 * HS), bf16),
            ((2 * rows, 3 * HS), bf16),
        ],
        "attend",
    )
    results, ready = (), soft
    weights = (qkv_mine, qkv_other, proj_mine, proj_other, attended)
    parts = [((HS, half // 2), bf16)] * 2
    given = [((rows, HS), bf16), ((rows, 2 * HS), bf16)]
    for backward, blocks, arrived in ((1, far_blocks, far), (0, near_blocks, near)):
        count = len(arrived)
        if backward:
            *arrived, ready = lax.optimization_barrier((*arrived, ready))
            local, shared, *others = on_device(
                functools.partial(arrive_kernel, backward, blocks, blocks, count, False, True),
                (parity,),
                (*arrived, *weights),
                given + parts,
                "arrive",
            )
            others = [swapped(piece) for piece in others]
        else:
            early, last = arrived
            early, ready = lax.optimization_barrier((early, ready))
            sums, *others = on_device(
                functools.partial(
                    arrive_kernel, backward, blocks[:-1], (), 1, False, False
                ),
                (parity,),
                (early, *weights),
                [((rows, HS), f32)] + parts,
                "begin",
            )
            others = [swapped(piece) for piece in others]
            last, sums = lax.optimization_barrier((last, sums))
            local, shared = on_device(
                functools.partial(
                    arrive_kernel, backward, blocks[-1:], blocks, count, True, True
                ),
                (parity,),
                (early, last, *weights, sums),
                given,
                "arrive",
            )
            arrived = [early, last]
        shared_other = swapped(shared)
        part, part_proj = on_device(
            functools.partial(own_kernel, backward, blocks, count, len(others)),
            (parity,),
            (*arrived, *others, local, shared, attended, soft, *padded),
            [((2 * rows, 3 * HS), f32), ((HS, half), bf16)],
            "own",
        )
        inputs = (
            *arrived,
            reads,
            part,
            shared_other,
            local,
            shared,
            proj_mine,
            proj_other,
            part_proj,
            qkv_mine,
            qkv_other,
            stashed,
            attended,
            normed,
            wide,
            inverse,
            soft,
            *padded,
        )
        results = pl.pallas_call(
            functools.partial(
                finish_kernel, backward, blocks, count, len(results)
            ),
            out_shape=[
                jax.ShapeDtypeStruct(shape, bf16)
                for shape in ((rows, features), (rows, features), (3 * HS, half), (HS, half))
            ],
            in_specs=[pl.BlockSpec(memory_space=pltpu.SMEM)] * 2
            + [pl.BlockSpec(memory_space=pltpu.VMEM)] * len(inputs)
            + [pl.BlockSpec(memory_space=pl.ANY)] * len(results),
            out_specs=[pl.BlockSpec(memory_space=pl.ANY)] * 4,
            scratch_shapes=[
                pltpu.VMEM((rows, features), bf16),
                pltpu.VMEM((3 * HS, half), bf16),
                pltpu.SemaphoreType.DMA((4,)),
            ],
            input_output_aliases={
                2 + len(inputs) + index: index for index in range(len(results))
            },
            compiler_params=pltpu.CompilerParams(vmem_limit_bytes=VMEM_LIMIT),
            cost_estimate=COST,
            name="finish",
        )(core, parity, *in_vmem(inputs), *results)
        ready = results[0]
    next_acts, next_grads, grad_qkv, grad_proj = results
    return (next_acts, next_grads, grad_qkv.T[None], grad_proj[None])


def solution(mesh):
    return jax.shard_map(
        per_device,
        mesh=mesh,
        in_specs=(
            P(("groups", "section", "shard"), None),
            P(("groups", "section", "shard"), None),
            P(("groups", "section", "shard"), None),
            P("section", "shard", None),
            P("section", None, "shard"),
            P(("groups", "section", "shard")),
        ),
        out_specs=(
            P(("groups", "section", "shard"), None),
            P(("groups", "section", "shard"), None),
            P(("groups", "section"), "shard", None),
            P(("groups", "section"), None, "shard"),
        ),
        check_vma=False,
    )
```
